32 devices in a mesh: groups: 2 (over y), team: 4 (over z), rep: 4 (over x, core).
Axes of the slice: x: 2, y: 2, z: 4, core: 2. Of those that a mesh axis runs over, the one named last changes fastest.
Arguments:
- omega_rows: float32 [128, 32768], P(('groups', 'team'), 'rep'), parts along dimension 0, as said below
- covariance_columns: float32 [32768, 2048], P('rep', ('groups', 'team')), parts along dimension 1, may hold values from -0.03125 to 0.03125
- tile_offsets: int32 [8], P(('groups', 'team')), parts along dimension 0, may hold values from 0 to 32512, as said below
Outputs:
- new_omega: float32 [64, 2048], P('rep', ('groups', 'team')), parts along dimension 1
The draws below stay inside these ranges and needn't reach their ends.
There are 2 independent parts, one for each index of `groups`. The reference program is written for one: setup_inputs(seed, part) draws one part's arguments, and reference() takes and returns one part's arrays. A program takes and returns all parts, laid end to end along the dimension named above; each array names one. Nothing has to cross between parts.
Inputs may be any that keep to these rules, and one draw needn't show every extreme that they name: `tile_offsets`: distinct multiples of 256; both 0 and 32512 occur. `omega_rows`: entries with column equal to row lie in 1 to 2.
All inputs are finite; a program needn't handle non-finite values.
Results may differ from the reference program's by a relative error of at most 0.0003.
Values sent between devices are 32-bit elements; how exact they have to be, the bound alone decides.
No kernel may reach another device: no remote copies, remote signals or barrier semaphores. Data moves between devices by JAX's collectives and lax.ppermute only.
A program may use at most 64 MiB of HBM per device.

```python
import jax
import jax.numpy as jnp
from jax import lax

P_SIZE = 32768
CB = 256
ROWS = 64
COLS = 1024
N_TEAM = 4


def draw_omega_rows(key, part):
    first_key = jax.random.fold_in(key, 11)
    second_key = jax.random.fold_in(key, 12)
    values = jax.random.normal(first_key, (ROWS, P_SIZE), jnp.float32)
    lifted = 1.0 + jax.random.uniform(second_key, (ROWS, P_SIZE), jnp.float32)
    row_ids = jnp.arange(ROWS, dtype=jnp.int32)[:, None]
    col_ids = jnp.arange(P_SIZE, dtype=jnp.int32)[None, :]
    return jnp.where(row_ids == col_ids, lifted, values)


def draw_tile_offsets(key, part):
    levels = P_SIZE // CB
    first_key = jax.random.fold_in(key, 21)
    second_key = jax.random.fold_in(key, 22)
    middle = jax.random.permutation(first_key, levels - 2)[:N_TEAM - 2] + 1
    chosen = jnp.concatenate([jnp.zeros((1,), jnp.int32), middle.astype(jnp.int32), jnp.full((1,), levels - 1, jnp.int32)])
    order = jax.random.permutation(second_key, N_TEAM)
    return (chosen[order] * CB).astype(jnp.int32)


def block_levels(stream_key, dims, pieces, least, top_value):
    gain = 1.0
    for position, shards_of in pieces:
        heights = jax.random.uniform(jax.random.fold_in(jax.random.fold_in(stream_key, 6), position), (shards_of,), jnp.float32, least / len(pieces), top_value / len(pieces))
        gain = gain * jnp.repeat(jnp.exp(heights), dims[position] // shards_of).reshape((-1,) + (1,) * (len(dims) - 1 - position))
    return gain


def normal_values(key, shape, spread, bound, split=(), kind=jnp.bfloat16):
    values = spread * jax.random.normal(key, shape, jnp.float32)
    if split:
        values = values * block_levels(key, shape, split, -0.22, 0.18)
    return jnp.clip(values, -bound, bound).astype(kind)


def setup_inputs(seed: int = 0, part: int = 0) -> dict:
    seeds = jax.random.split(jax.random.key(seed), 4)
    part_keys = jax.random.split(jax.random.fold_in(seeds[3], part), 4)
    omega_rows = draw_omega_rows(jax.random.fold_in(jax.random.fold_in(seeds[3], part), 71), part)
    covariance_columns = normal_values(part_keys[1], (P_SIZE, COLS), P_SIZE ** -0.5, 0.03125, ((0, 4), (1, 4)), jnp.float32)
    tile_offsets = draw_tile_offsets(jax.random.fold_in(jax.random.fold_in(seeds[3], part), 71), part)
    return {"omega_rows": omega_rows, "covariance_columns": covariance_columns, "tile_offsets": tile_offsets}


step_size = 0.5
penalty = 0.1


def reference(omega_rows, covariance_columns, tile_offsets):
    columns = (tile_offsets[:, None] + jnp.arange(CB, dtype=jnp.int32)[None, :]).reshape(-1).astype(jnp.int32)
    product = jnp.dot(omega_rows, covariance_columns, preferred_element_type=jnp.float32, precision=lax.Precision.HIGHEST)
    current = jnp.take(omega_rows, columns, axis=1)
    row_ids = jnp.arange(ROWS, dtype=jnp.int32)[:, None]
    diagonal = row_ids == columns[None, :]
    safe = jnp.where(diagonal, current, jnp.float32(1.0))
    gradient = product - jnp.where(diagonal, 1.0 / safe, jnp.float32(0.0))
    moved = current - step_size * gradient
    shrunk = jnp.sign(moved) * jnp.maximum(jnp.abs(moved) - step_size * penalty, 0.0)
    return jnp.where(diagonal, moved, shrunk)
```

```python
import jax
import jax.numpy as jnp
from jax import lax
from jax.sharding import PartitionSpec as P

step_size = 0.5
penalty = 0.1
largest_bf16 = 3.3895313892515355e38


def halves(array):
    high = lax.reduce_precision(jnp.clip(array, -largest_bf16, largest_bf16), 8, 7)
    return high.astype(jnp.bfloat16), (array - high).astype(jnp.bfloat16)


def product_of(block, weights):
    high, low = halves(block)
    rows = block.shape[0]
    both = jnp.dot(
        jnp.concatenate([high, low], 0), weights[0], preferred_element_type=jnp.float32
    )
    cross = jnp.dot(high, weights[1], preferred_element_type=jnp.float32)
    return both[:rows] + both[rows:] + cross


def sum_of(terms):
    total = terms[0]
    for term in terms[1:]:
        total = total + term
    return total


def per_device(omega_rows, covariance_columns, tile_offsets):
    team_count = lax.axis_size("team")
    rep_count = lax.axis_size("rep")
    team_index = lax.axis_index("team")
    rep_index = lax.axis_index("rep")
    block_rows, part_width = omega_rows.shape
    tile_width = covariance_columns.shape[1]
    all_rows = block_rows * team_count
    rows_share = all_rows // rep_count
    offset = tile_offsets[0]
    chunks = 2 if team_count <= 4 else 1
    width = part_width // chunks
    assert all_rows <= width and width % tile_width == 0

    weights = []
    for c in range(chunks):
        columns = covariance_columns[c * width : (c + 1) * width]
        k_ids = rep_index * part_width + c * width + jnp.arange(width, dtype=jnp.int32)
        c_ids = offset + jnp.arange(tile_width, dtype=jnp.int32)
        chosen = (k_ids[:, None] == c_ids[None, :]).astype(jnp.float32)
        weights.append(halves(chosen - step_size * columns))

    def inverse_diagonal(first_chunk, source):
        start = jnp.clip(offset, 0, width - tile_width)
        values = lax.dynamic_slice_in_dim(first_chunk, start, tile_width, 1)
        row_ids = source * block_rows + jnp.arange(block_rows, dtype=jnp.int32)
        c_ids = offset + jnp.arange(tile_width, dtype=jnp.int32)
        mask = (row_ids[:, None] == c_ids[None, :]) & (rep_index == 0)
        return jnp.where(mask, step_size / jnp.where(mask, values, 1.0), 0.0)

    own = [omega_rows[:, c * width : (c + 1) * width] for c in range(chunks)]
    slots = []

    def add_slot(parts, source, valid):
        terms = [product_of(parts[c], weights[c]) for c in range(chunks)]
        terms.append(inverse_diagonal(parts[0], source))
        slots.append((sum_of(terms), jnp.where(valid, source, -1)))

    add_slot(own, team_index, True)
    right, left = own, own
    for step in range(1, team_count):
        to_right = [(d, d + 1) for d in range(step - 1, team_count - 1)]
        to_left = [(d, d - 1) for d in range(1, team_count - step + 1)]
        right, left = (
            [lax.ppermute(part, "team", to_right) for part in right],
            [lax.ppermute(part, "team", to_left) for part in left],
        )
        from_left = team_index >= step
        if 2 * step < team_count:
            add_slot(right, team_index - step, from_left)
            add_slot(left, team_index + step, team_index + step < team_count)
        else:
            merged = [jnp.where(from_left, r, l) for r, l in zip(right, left)]
            source = jnp.where(from_left, team_index - step, team_index + step)
            add_slot(merged, source, from_left | (source < team_count))

    blocks = []
    for b in range(team_count):
        value = jnp.zeros((block_rows, tile_width), jnp.float32)
        for slot, source in slots:
            value = jnp.where(source == b, slot, value)
        blocks.append(value)
    partial_moved = jnp.concatenate(blocks, 0)

    terms = []
    for by in range(rep_count):
        target = (rep_index + by) % rep_count
        part = lax.dynamic_slice_in_dim(partial_moved, target * rows_share, rows_share, 0)
        if by:
            pairs = [(d, (d + by) % rep_count) for d in range(rep_count)]
            part = lax.ppermute(part, "rep", pairs)
        terms.append(part)
    moved = sum_of(terms)

    global_rows = rep_index * rows_share + jnp.arange(rows_share, dtype=jnp.int32)
    global_cols = offset + jnp.arange(tile_width, dtype=jnp.int32)
    diagonal = global_rows[:, None] == global_cols[None, :]
    shrunk = jnp.sign(moved) * jnp.maximum(jnp.abs(moved) - step_size * penalty, 0.0)
    return jnp.where(diagonal, moved, shrunk)


def solution(mesh):
    in_specs = (P(("groups", "team"), "rep"), P("rep", ("groups", "team")), P(("groups", "team")))
    out_specs = P("rep", ("groups", "team"))
    return jax.shard_map(
        per_device, mesh=mesh, in_specs=in_specs, out_specs=out_specs, check_vma=False
    )
```

```python
import jax
import jax.numpy as jnp
from jax import lax
from jax.sharding import PartitionSpec as P

step_size = 0.5
penalty = 0.1
largest_bf16 = 3.3895313892515355e38


def halves(array):
    high = lax.reduce_precision(jnp.clip(array, -largest_bf16, largest_bf16), 8, 7)
    return high.astype(jnp.bfloat16), (array - high).astype(jnp.bfloat16)


def product_of(block, weights):
    high, low = halves(block)
    rows = block.shape[0]
    both = jnp.dot(
        jnp.concatenate([high, low], 0), weights[0], preferred_element_type=jnp.float32
    )
    cross = jnp.dot(high, weights[1], preferred_element_type=jnp.float32)
    return both[:rows] + both[rows:] + cross


def sum_of(terms):
    total = terms[0]
    for term in terms[1:]:
        total = total + term
    return total


def per_device(omega_rows, covariance_columns, tile_offsets):
    team_count = lax.axis_size("team")
    rep_count = lax.axis_size("rep")
    team_index = lax.axis_index("team")
    rep_index = lax.axis_index("rep")
    block_rows, part_width = omega_rows.shape
    tile_width = covariance_columns.shape[1]
    all_rows = block_rows * team_count
    rows_share = all_rows // rep_count
    offset = tile_offsets[0]
    assert all_rows <= part_width and part_width % tile_width == 0

    k_ids = rep_index * part_width + jnp.arange(part_width, dtype=jnp.int32)
    c_ids = offset + jnp.arange(tile_width, dtype=jnp.int32)
    chosen = (k_ids[:, None] == c_ids[None, :]).astype(jnp.float32)
    weights = halves(chosen - step_size * covariance_columns)

    def inverse_diagonal(block, source):
        start = jnp.clip(offset, 0, part_width - tile_width)
        values = lax.dynamic_slice_in_dim(block, start, tile_width, 1)
        row_ids = source * block_rows + jnp.arange(block_rows, dtype=jnp.int32)
        mask = (row_ids[:, None] == c_ids[None, :]) & (rep_index == 0)
        return jnp.where(mask, step_size / jnp.where(mask, values, 1.0), 0.0)

    slots = []

    def add_slot(block, source, valid=True):
        moved_part = product_of(block, weights) + inverse_diagonal(block, source)
        slots.append((moved_part, jnp.where(valid, source, -1)))

    add_slot(omega_rows, team_index)
    if team_count == 4:
        across = lax.ppermute(omega_rows, "team", [(0, 2), (1, 3), (2, 0), (3, 1)])
        pair = lax.ppermute(omega_rows, "team", [(0, 1), (1, 0), (2, 3), (3, 2)])
        passed = lax.ppermute(across, "team", [(1, 0), (2, 3)])
        own_later, _ = lax.optimization_barrier((omega_rows, across))
        middle = lax.ppermute(own_later, "team", [(1, 2), (2, 1)])
        add_slot(across, (team_index + 2) % 4)
        add_slot(pair, team_index ^ 1)
        is_end = (team_index == 0) | (team_index == 3)
        add_slot(jnp.where(is_end, passed, middle), 3 - team_index)
    else:
        right, left = omega_rows, omega_rows
        for step in range(1, team_count):
            to_right = [(d, d + 1) for d in range(step - 1, team_count - 1)]
            to_left = [(d, d - 1) for d in range(1, team_count - step + 1)]
            right = lax.ppermute(right, "team", to_right)
            left = lax.ppermute(left, "team", to_left)
            from_left = team_index >= step
            from_right = team_index + step < team_count
            if 2 * step < team_count:
                add_slot(right, team_index - step, from_left)
                add_slot(left, team_index + step, from_right)
            else:
                merged = jnp.where(from_left, right, left)
                source = jnp.where(from_left, team_index - step, team_index + step)
                add_slot(merged, source, from_left | from_right)

    blocks = []
    for b in range(team_count):
        value = jnp.zeros((block_rows, tile_width), jnp.float32)
        for slot, source in slots:
            value = jnp.where(source == b, slot, value)
        blocks.append(value)
    partial_moved = jnp.concatenate(blocks, 0)

    terms = []
    for by in range(rep_count):
        target = (rep_index + by) % rep_count
        part = lax.dynamic_slice_in_dim(partial_moved, target * rows_share, rows_share, 0)
        if by:
            pairs = [(d, (d + by) % rep_count) for d in range(rep_count)]
            part = lax.ppermute(part, "rep", pairs)
        terms.append(part)
    moved = sum_of(terms)

    global_rows = rep_index * rows_share + jnp.arange(rows_share, dtype=jnp.int32)
    global_cols = offset + jnp.arange(tile_width, dtype=jnp.int32)
    diagonal = global_rows[:, None] == global_cols[None, :]
    shrunk = jnp.sign(moved) * jnp.maximum(jnp.abs(moved) - step_size * penalty, 0.0)
    return jnp.where(diagonal, moved, shrunk)


def solution(mesh):
    in_specs = (P(("groups", "team"), "rep"), P("rep", ("groups", "team")), P(("groups", "team")))
    out_specs = P("rep", ("groups", "team"))
    return jax.shard_map(
        per_device, mesh=mesh, in_specs=in_specs, out_specs=out_specs, check_vma=False
    )
```

```python
import jax
import jax.numpy as jnp
from jax import lax
from jax.sharding import PartitionSpec as P

step_size = 0.5
penalty = 0.1
largest_bf16 = 3.3895313892515355e38


def halves(array):
    high = lax.reduce_precision(jnp.clip(array, -largest_bf16, largest_bf16), 8, 7)
    return high.astype(jnp.bfloat16), (array - high).astype(jnp.bfloat16)


def product_of(block, weights):
    high, low = halves(block)
    rows = block.shape[0]
    both = jnp.dot(
        jnp.concatenate([high, low], 0), weights[0], preferred_element_type=jnp.float32
    )
    cross = jnp.dot(high, weights[1], preferred_element_type=jnp.float32)
    return both[:rows] + both[rows:] + cross


def sum_of(terms):
    total = terms[0]
    for term in terms[1:]:
        total = total + term
    return total


def per_device(omega_rows, covariance_columns, tile_offsets):
    team_count = lax.axis_size("team")
    rep_count = lax.axis_size("rep")
    team_index = lax.axis_index("team")
    rep_index = lax.axis_index("rep")
    block_rows, part_width = omega_rows.shape
    tile_width = covariance_columns.shape[1]
    all_rows = block_rows * team_count
    rows_share = all_rows // rep_count
    offset = tile_offsets[0]
    assert all_rows <= part_width and part_width % tile_width == 0

    k_ids = rep_index * part_width + jnp.arange(part_width, dtype=jnp.int32)
    c_ids = offset + jnp.arange(tile_width, dtype=jnp.int32)
    chosen = (k_ids[:, None] == c_ids[None, :]).astype(jnp.float32)
    weights = halves(chosen - step_size * covariance_columns)

    def inverse_diagonal(block, source):
        start = jnp.clip(offset, 0, part_width - tile_width)
        values = lax.dynamic_slice_in_dim(block, start, tile_width, 1)
        row_ids = source * block_rows + jnp.arange(block_rows, dtype=jnp.int32)
        mask = (row_ids[:, None] == c_ids[None, :]) & (rep_index == 0)
        return jnp.where(mask, step_size / jnp.where(mask, values, 1.0), 0.0)

    slots = []

    def add_slot(block, source):
        moved_part = product_of(block, weights) + inverse_diagonal(block, source)
        slots.append((moved_part, source))

    ring = list(range(0, team_count, 2)) + list(range(1, team_count, 2))[::-1]
    onward = [(ring[k], ring[(k + 1) % team_count]) for k in range(team_count)]
    backward = [(to, source) for source, to in onward]
    half = team_index // 2
    place = jnp.where(team_index % 2 == 0, half, team_count - 1 - half)

    def device_at(spot):
        spot = spot % team_count
        up = 2 * spot
        return jnp.where(up < team_count, up, 2 * team_count - 1 - up)

    first = lax.ppermute(omega_rows, "team", onward)
    own, *weights = lax.optimization_barrier((omega_rows, *weights))
    gathered = [(own, 0), (first, 1)]
    held = first
    for step in range(2, team_count // 2 + 1):
        held = lax.ppermute(held, "team", onward)
        gathered.append((held, step))
    held = own
    for step in range(1, team_count - team_count // 2):
        held = lax.ppermute(held, "team", backward)
        gathered.append((held, -step))
    for block, step in gathered:
        add_slot(block, device_at(place - step))

    blocks = []
    for b in range(team_count):
        value = jnp.zeros((block_rows, tile_width), jnp.float32)
        for slot, source in slots:
            value = jnp.where(source == b, slot, value)
        blocks.append(value)
    partial_moved = jnp.concatenate(blocks, 0)

    terms = []
    for by in range(rep_count):
        target = (rep_index + by) % rep_count
        part = lax.dynamic_slice_in_dim(partial_moved, target * rows_share, rows_share, 0)
        if by:
            pairs = [(d, (d + by) % rep_count) for d in range(rep_count)]
            part = lax.ppermute(part, "rep", pairs)
        terms.append(part)
    moved = sum_of(terms)

    global_rows = rep_index * rows_share + jnp.arange(rows_share, dtype=jnp.int32)
    global_cols = offset + jnp.arange(tile_width, dtype=jnp.int32)
    diagonal = global_rows[:, None] == global_cols[None, :]
    shrunk = jnp.sign(moved) * jnp.maximum(jnp.abs(moved) - step_size * penalty, 0.0)
    return jnp.where(diagonal, moved, shrunk)


def solution(mesh):
    in_specs = (P(("groups", "team"), "rep"), P("rep", ("groups", "team")), P(("groups", "team")))
    out_specs = P("rep", ("groups", "team"))
    return jax.shard_map(
        per_device, mesh=mesh, in_specs=in_specs, out_specs=out_specs, check_vma=False
    )
```

```python
import math

import jax
import jax.numpy as jnp
from jax import lax
from jax.experimental import pallas as pl
from jax.experimental.pallas import tpu as pltpu
from jax.sharding import PartitionSpec as P

step_size = 0.5
penalty = 0.1
largest_bf16 = 3.3895313892515355e38


def halves(array):
    high = lax.reduce_precision(jnp.clip(array, -largest_bf16, largest_bf16), 8, 7)
    return high.astype(jnp.bfloat16), (array - high).astype(jnp.bfloat16)


def slot_kernel(places, block, high, low, out):
    rows, depth = block.shape
    columns = high.shape[1]
    step = math.gcd(depth, 2048)
    total = jnp.zeros((rows, columns), jnp.float32)
    for k in range(0, depth, step):
        values = block[:, k : k + step]
        upper = jnp.clip(values, -largest_bf16, largest_bf16).astype(jnp.bfloat16)
        lower = (values - upper.astype(jnp.float32)).astype(jnp.bfloat16)
        both = jnp.concatenate([upper, lower], 0)
        main = jnp.dot(both, high[k : k + step], preferred_element_type=jnp.float32)
        cross = jnp.dot(upper, low[k : k + step], preferred_element_type=jnp.float32)
        total += main[:rows] + main[rows:] + cross
    current = block[:, pl.ds(pl.multiple_of(places[0], columns), columns)]
    row_ids = lax.broadcasted_iota(jnp.int32, (rows, columns), 0) + places[1]
    mask = row_ids == lax.broadcasted_iota(jnp.int32, (rows, columns), 1)
    out[...] = total + jnp.where(mask, step_size / jnp.where(mask, current, 1.0), 0.0)


def slot_product(places, block, weights):
    rows, columns = block.shape[0], weights[0].shape[1]
    return pl.pallas_call(
        slot_kernel,
        out_shape=jax.ShapeDtypeStruct((rows, columns), jnp.float32),
        in_specs=[pl.BlockSpec(memory_space=pltpu.SMEM)]
        + [pl.BlockSpec(memory_space=pltpu.VMEM)] * 3,
        out_specs=pl.BlockSpec(memory_space=pltpu.VMEM),
        compiler_params=pltpu.CompilerParams(vmem_limit_bytes=32 * 1024 * 1024),
        cost_estimate=pl.CostEstimate(flops=0, bytes_accessed=block.size * 4, transcendentals=0),
    )(places, block, *weights)


def sum_of(terms):
    total = terms[0]
    for term in terms[1:]:
        total = total + term
    return total


def per_device(omega_rows, covariance_columns, tile_offsets):
    team_count = lax.axis_size("team")
    rep_count = lax.axis_size("rep")
    team_index = lax.axis_index("team")
    rep_index = lax.axis_index("rep")
    block_rows, part_width = omega_rows.shape
    tile_width = covariance_columns.shape[1]
    all_rows = block_rows * team_count
    rows_share = all_rows // rep_count
    offset = tile_offsets[0]
    assert all_rows <= part_width and part_width % tile_width == 0
    assert rows_share % block_rows == 0

    k_ids = rep_index * part_width + jnp.arange(part_width, dtype=jnp.int32)
    c_ids = offset + jnp.arange(tile_width, dtype=jnp.int32)
    chosen = (k_ids[:, None] == c_ids[None, :]).astype(jnp.float32)
    weights = halves(chosen - step_size * covariance_columns)

    def part_of(block, source):
        start = jnp.clip(offset, 0, part_width - tile_width)
        shift = jnp.where(rep_index == 0, source * block_rows - offset, 1 << 20)
        return slot_product(jnp.stack([start, shift]).astype(jnp.int32), block, weights)

    slots = []

    ring = list(range(0, team_count, 2)) + list(range(1, team_count, 2))[::-1]
    onward = [(ring[k], ring[(k + 1) % team_count]) for k in range(team_count)]
    backward = [(to, source) for source, to in onward]
    half = team_index // 2
    place = jnp.where(team_index % 2 == 0, half, team_count - 1 - half)

    def device_at(spot):
        spot = spot % team_count
        up = 2 * spot
        return jnp.where(up < team_count, up, 2 * team_count - 1 - up)

    first = lax.ppermute(omega_rows, "team", onward)
    own, *weights = lax.optimization_barrier((omega_rows, *weights))
    last_step = team_count // 2
    gathered = [(own, 0), (first, 1)]
    held = first
    for step in range(2, last_step + 1):
        held = lax.ppermute(held, "team", onward)
        gathered.append((held, step))
    last = held
    held = own
    for step in range(1, team_count - last_step):
        held = lax.ppermute(held, "team", backward)
        gathered.append((held, -step))
    for block, step in gathered:
        if step != last_step:
            source = device_at(place - step)
            slots.append((part_of(block, source), source))

    blocks = []
    for b in range(team_count):
        value = jnp.zeros((block_rows, tile_width), jnp.float32)
        for slot, source in slots:
            value = jnp.where(source == b, slot, value)
        blocks.append(value)
    partial_moved = jnp.concatenate(blocks, 0)

    terms = []
    for by in range(rep_count):
        target = (rep_index + by) % rep_count
        part = lax.dynamic_slice_in_dim(partial_moved, target * rows_share, rows_share, 0)
        if by:
            pairs = [(d, (d + by) % rep_count) for d in range(rep_count)]
            part = lax.ppermute(part, "rep", pairs)
        terms.append(part)

    last_source = device_at(place - last_step)
    last_part = part_of(last, last_source)
    share_blocks = rows_share // block_rows
    roots = [
        ring[(ring.index(d) - last_step) % team_count] // share_blocks for d in range(team_count)
    ]
    late = last_part
    for by in range(1, rep_count):
        pairs = [
            (d * rep_count + (roots[d] + by) % rep_count, d * rep_count + roots[d])
            for d in range(team_count)
        ]
        late = late + lax.ppermute(last_part, ("team", "rep"), pairs)
    late_place = jnp.where(
        last_source // share_blocks == rep_index, last_source % share_blocks, -1
    )
    late_blocks = [jnp.where(late_place == b, late, 0.0) for b in range(share_blocks)]
    moved = sum_of(terms) + jnp.concatenate(late_blocks, 0)

    global_rows = rep_index * rows_share + jnp.arange(rows_share, dtype=jnp.int32)
    global_cols = offset + jnp.arange(tile_width, dtype=jnp.int32)
    diagonal = global_rows[:, None] == global_cols[None, :]
    shrunk = jnp.sign(moved) * jnp.maximum(jnp.abs(moved) - step_size * penalty, 0.0)
    return jnp.where(diagonal, moved, shrunk)


def solution(mesh):
    in_specs = (P(("groups", "team"), "rep"), P("rep", ("groups", "team")), P(("groups", "team")))
    out_specs = P("rep", ("groups", "team"))
    return jax.shard_map(
        per_device, mesh=mesh, in_specs=in_specs, out_specs=out_specs, check_vma=False
    )
```

```python
import math

import jax
import jax.numpy as jnp
from jax import lax
from jax.experimental import pallas as pl
from jax.experimental.pallas import tpu as pltpu
from jax.sharding import PartitionSpec as P

step_size = 0.5
penalty = 0.1
largest_bf16 = 3.3895313892515355e38


def halves(array):
    high = lax.reduce_precision(jnp.clip(array, -largest_bf16, largest_bf16), 8, 7)
    return high.astype(jnp.bfloat16), (array - high).astype(jnp.bfloat16)


def slot_kernel(places, block, high, low, *rest):
    *others, out = rest
    rows, depth = block.shape
    columns = high.shape[1]
    step = math.gcd(depth, 2048)
    total = jnp.zeros((rows, columns), jnp.float32)
    for k in range(0, depth, step):
        values = block[:, k : k + step]
        upper = jnp.clip(values, -largest_bf16, largest_bf16).astype(jnp.bfloat16)
        lower = (values - upper.astype(jnp.float32)).astype(jnp.bfloat16)
        both = jnp.concatenate([upper, lower], 0)
        main = jnp.dot(both, high[k : k + step], preferred_element_type=jnp.float32)
        cross = jnp.dot(upper, low[k : k + step], preferred_element_type=jnp.float32)
        total += main[:rows] + main[rows:] + cross
    current = block[:, pl.ds(pl.multiple_of(places[0], columns), columns)]
    row_ids = lax.broadcasted_iota(jnp.int32, (rows, columns), 0) + places[1]
    mask = row_ids == lax.broadcasted_iota(jnp.int32, (rows, columns), 1)
    total += jnp.where(mask, step_size / jnp.where(mask, current, 1.0), 0.0)
    if not others:
        out[...] = total
        return
    for position, part in enumerate(others):
        out[places[2 + position]] = part[...]
    out[places[2 + len(others)]] = total


def slot_product(places, block, weights, others=()):
    rows, columns = block.shape[0], weights[0].shape[1]
    shape = (len(others) + 1, rows, columns) if others else (rows, columns)
    return pl.pallas_call(
        slot_kernel,
        out_shape=jax.ShapeDtypeStruct(shape, jnp.float32),
        in_specs=[pl.BlockSpec(memory_space=pltpu.SMEM)]
        + [pl.BlockSpec(memory_space=pltpu.VMEM)] * (3 + len(others)),
        out_specs=pl.BlockSpec(memory_space=pltpu.VMEM),
        compiler_params=pltpu.CompilerParams(vmem_limit_bytes=2 * 1024 * 1024),
        cost_estimate=pl.CostEstimate(flops=0, bytes_accessed=block.size * 4, transcendentals=0),
    )(places, block, *weights, *others)


def sum_of(terms):
    total = terms[0]
    for term in terms[1:]:
        total = total + term
    return total


def per_device(omega_rows, covariance_columns, tile_offsets):
    team_count = lax.axis_size("team")
    rep_count = lax.axis_size("rep")
    team_index = lax.axis_index("team")
    rep_index = lax.axis_index("rep")
    block_rows, part_width = omega_rows.shape
    tile_width = covariance_columns.shape[1]
    all_rows = block_rows * team_count
    rows_share = all_rows // rep_count
    offset = tile_offsets[0]
    assert all_rows <= part_width and part_width % tile_width == 0
    assert rows_share % block_rows == 0

    k_ids = rep_index * part_width + jnp.arange(part_width, dtype=jnp.int32)
    c_ids = offset + jnp.arange(tile_width, dtype=jnp.int32)
    chosen = (k_ids[:, None] == c_ids[None, :]).astype(jnp.float32)
    weights = halves(chosen - step_size * covariance_columns)

    def part_of(block, source, others=(), sources=()):
        start = jnp.clip(offset, 0, part_width - tile_width)
        shift = jnp.where(rep_index == 0, source * block_rows - offset, 1 << 20)
        places = jnp.stack([start, shift, *sources]).astype(jnp.int32)
        return slot_product(places, block, weights, others)

    ring = list(range(0, team_count, 2)) + list(range(1, team_count, 2))[::-1]
    onward = [(ring[k], ring[(k + 1) % team_count]) for k in range(team_count)]
    backward = [(to, source) for source, to in onward]
    half = team_index // 2
    place = jnp.where(team_index % 2 == 0, half, team_count - 1 - half)

    def device_at(spot):
        spot = spot % team_count
        up = 2 * spot
        return jnp.where(up < team_count, up, 2 * team_count - 1 - up)

    first = lax.ppermute(omega_rows, "team", onward)
    own, *weights = lax.optimization_barrier((omega_rows, *weights))
    last_step = team_count // 2
    gathered = [(own, 0), (first, 1)]
    held = first
    for step in range(2, last_step + 1):
        held = lax.ppermute(held, "team", onward)
        gathered.append((held, step))
    last = held
    held = own
    for step in range(1, team_count - last_step):
        held = lax.ppermute(held, "team", backward)
        gathered.append((held, -step))
    others, sources = [], []
    for block, step in gathered:
        if step != last_step:
            source = device_at(place - step)
            others.append(part_of(block, source))
            sources.append(source)
    source = device_at(place - last_step)
    partial_moved = part_of(last, source, others, sources + [source])

    shares = partial_moved.reshape(rep_count, rows_share, tile_width)
    shares = lax.all_to_all(shares, "rep", 0, 0)
    moved = sum_of([shares[r] for r in range(rep_count)])

    global_rows = rep_index * rows_share + jnp.arange(rows_share, dtype=jnp.int32)
    global_cols = offset + jnp.arange(tile_width, dtype=jnp.int32)
    diagonal = global_rows[:, None] == global_cols[None, :]
    shrunk = jnp.sign(moved) * jnp.maximum(jnp.abs(moved) - step_size * penalty, 0.0)
    return jnp.where(diagonal, moved, shrunk)


def solution(mesh):
    in_specs = (P(("groups", "team"), "rep"), P("rep", ("groups", "team")), P(("groups", "team")))
    out_specs = P("rep", ("groups", "team"))
    return jax.shard_map(
        per_device, mesh=mesh, in_specs=in_specs, out_specs=out_specs, check_vma=False
    )
```

```python
import functools
import math

import jax
import jax.numpy as jnp
from jax import lax
from jax.experimental import pallas as pl
from jax.experimental.pallas import tpu as pltpu
from jax.sharding import PartitionSpec as P

step_size = 0.5
penalty = 0.1
largest_bf16 = 3.3895313892515355e38


def halves(array):
    high = lax.reduce_precision(jnp.clip(array, -largest_bf16, largest_bf16), 8, 7)
    return high.astype(jnp.bfloat16), (array - high).astype(jnp.bfloat16)


def slot_kernel(first_k, parts, places, block, high, low, *rest):
    others, outs = rest[:parts], rest[parts:]
    rows, depth = block.shape
    columns = high.shape[1]
    step = math.gcd(depth, 4096)
    total = jnp.zeros((rows, columns), jnp.float32)
    for k in range(0, depth, step):
        values = block[:, k : k + step]
        upper = jnp.clip(values, -largest_bf16, largest_bf16).astype(jnp.bfloat16)
        lower = (values - upper.astype(jnp.float32)).astype(jnp.bfloat16)
        both = jnp.concatenate([upper, lower], 0)
        span = slice(first_k + k, first_k + k + step)
        main = jnp.dot(both, high[span], preferred_element_type=jnp.float32)
        cross = jnp.dot(upper, low[span], preferred_element_type=jnp.float32)
        total += main[:rows] + main[rows:] + cross
    if first_k == 0:
        current = block[:, pl.ds(pl.multiple_of(places[0], columns), columns)]
        row_ids = lax.broadcasted_iota(jnp.int32, (rows, columns), 0) + places[1]
        mask = row_ids == lax.broadcasted_iota(jnp.int32, (rows, columns), 1)
        total += jnp.where(mask, step_size / jnp.where(mask, current, 1.0), 0.0)
    if not parts:
        outs[0][...] = total
        return
    values = [part[...] for part in others]
    values[-1] += total
    per_share = outs[0].shape[0] // rows
    for share, out in enumerate(outs):
        for b in range(per_share):
            found = jnp.zeros((rows, columns), jnp.float32)
            for part, value in enumerate(values):
                found = jnp.where(places[2 + part] == share * per_share + b, value, found)
            out[b * rows : (b + 1) * rows] = found


def slot_product(places, block, weights, first_k=0, others=(), shares=1):
    rows, columns = block.shape[0], weights[0].shape[1]
    shape = (rows * max(len(others), 1) // shares, columns)
    return pl.pallas_call(
        functools.partial(slot_kernel, first_k, len(others)),
        out_shape=[jax.ShapeDtypeStruct(shape, jnp.float32)] * shares,
        in_specs=[pl.BlockSpec(memory_space=pltpu.SMEM)]
        + [pl.BlockSpec(memory_space=pltpu.VMEM)] * (3 + len(others)),
        out_specs=[pl.BlockSpec(memory_space=pltpu.VMEM)] * shares,
        compiler_params=pltpu.CompilerParams(vmem_limit_bytes=(2 + len(others) // 4) * 1024 * 1024),
        cost_estimate=pl.CostEstimate(flops=0, bytes_accessed=block.size * 4, transcendentals=0),
    )(places, block, *weights, *others)


def sum_of(terms):
    total = terms[0]
    for term in terms[1:]:
        total = total + term
    return total


def per_device(omega_rows, covariance_columns, tile_offsets):
    team_count = lax.axis_size("team")
    rep_count = lax.axis_size("rep")
    team_index = lax.axis_index("team")
    rep_index = lax.axis_index("rep")
    block_rows, part_width = omega_rows.shape
    tile_width = covariance_columns.shape[1]
    all_rows = block_rows * team_count
    rows_share = all_rows // rep_count
    offset = tile_offsets[0]
    assert all_rows <= part_width and part_width % tile_width == 0
    assert rows_share % block_rows == 0

    k_ids = rep_index * part_width + jnp.arange(part_width, dtype=jnp.int32)
    c_ids = offset + jnp.arange(tile_width, dtype=jnp.int32)
    chosen = (k_ids[:, None] == c_ids[None, :]).astype(jnp.float32)
    weights = halves(chosen - step_size * covariance_columns)

    half = part_width // 2
    assert all_rows <= half and half % tile_width == 0

    def places_of(source, *more):
        start = jnp.clip(offset, 0, half - tile_width)
        shift = jnp.where(rep_index == 0, source * block_rows - offset, 1 << 20)
        return jnp.stack([start, shift, *more]).astype(jnp.int32)

    ring = list(range(0, team_count, 2)) + list(range(1, team_count, 2))[::-1]
    onward = [(ring[k], ring[(k + 1) % team_count]) for k in range(team_count)]
    backward = [(to, source) for source, to in onward]
    rank = team_index // 2
    place = jnp.where(team_index % 2 == 0, rank, team_count - 1 - rank)

    def device_at(spot):
        spot = spot % team_count
        up = 2 * spot
        return jnp.where(up < team_count, up, 2 * team_count - 1 - up)

    first = lax.ppermute(omega_rows, "team", onward)
    own, *weights = lax.optimization_barrier((omega_rows, *weights))
    last_step = team_count // 2
    gathered = [(own, 0), (first, 1)]
    held = first
    for step in range(2, last_step):
        held = lax.ppermute(held, "team", onward)
        gathered.append((held, step))
    last_held = held
    held = own
    for step in range(1, team_count - last_step):
        held = lax.ppermute(held, "team", backward)
        gathered.append((held, -step))

    last_left = lax.ppermute(last_held[:, :half], "team", onward)
    others, sources = [], []
    for block, step in gathered:
        source = device_at(place - step)
        others += slot_product(places_of(source), block, weights)
        sources.append(source)
        if step == 1:
            last_held, others[-1] = lax.optimization_barrier((last_held, others[-1]))
    last_right = lax.ppermute(last_held[:, half:], "team", onward)
    source = device_at(place - last_step)
    others += slot_product(places_of(source), last_left, weights)
    sources.append(source)

    share_blocks = rows_share // block_rows
    spots = [(source - rep_index * share_blocks) % team_count for source in sources]
    shares = slot_product(
        places_of(source, *spots), last_right, weights, half, others, rep_count
    )
    terms = [shares[0]]
    for by in range(1, rep_count):
        pairs = [(d, (d + by) % rep_count) for d in range(rep_count)]
        terms.append(lax.ppermute(shares[by], "rep", pairs))
    moved = sum_of(terms)

    global_rows = rep_index * rows_share + jnp.arange(rows_share, dtype=jnp.int32)
    global_cols = offset + jnp.arange(tile_width, dtype=jnp.int32)
    diagonal = global_rows[:, None] == global_cols[None, :]
    shrunk = jnp.sign(moved) * jnp.maximum(jnp.abs(moved) - step_size * penalty, 0.0)
    return jnp.where(diagonal, moved, shrunk)


def solution(mesh):
    in_specs = (P(("groups", "team"), "rep"), P("rep", ("groups", "team")), P(("groups", "team")))
    out_specs = P("rep", ("groups", "team"))
    return jax.shard_map(
        per_device, mesh=mesh, in_specs=in_specs, out_specs=out_specs, check_vma=False
    )
```

```python
import functools
import math

import jax
import jax.numpy as jnp
from jax import lax
from jax.experimental import pallas as pl
from jax.experimental.pallas import tpu as pltpu
from jax.sharding import PartitionSpec as P

step_size = 0.5
penalty = 0.1
largest_bf16 = 3.3895313892515355e38


def weights_kernel(shift, covariance, high, low, held, arrived):
    depth, columns = covariance.shape
    step = held.shape[1]
    pieces = depth // step

    def copy(piece):
        return pltpu.make_async_copy(
            covariance.at[pl.ds(piece * step, step)], held.at[piece % 4], arrived.at[piece % 4]
        )

    for piece in range(min(3, pieces)):
        copy(piece).start()
    ahead = lax.broadcasted_iota(jnp.int32, (step, columns), 0)
    ahead -= lax.broadcasted_iota(jnp.int32, (step, columns), 1)
    for piece in range(pieces):
        if piece + 3 < pieces:
            copy(piece + 3).start()
        copy(piece).wait()
        scaled = -step_size * held[piece % 4]
        values = jnp.where(ahead == shift[0] - piece * step, scaled + 1.0, scaled)
        upper = values.astype(jnp.bfloat16)
        rows = slice(piece * step, (piece + 1) * step)
        high[rows] = upper
        low[rows] = (values - upper.astype(jnp.float32)).astype(jnp.bfloat16)


def weights_of(covariance, shift):
    depth, columns = covariance.shape
    step = math.gcd(depth, 512)
    return pl.pallas_call(
        weights_kernel,
        out_shape=[pltpu.VMEM((depth, columns), jnp.bfloat16)] * 2,
        in_specs=[
            pl.BlockSpec(memory_space=pltpu.SMEM),
            pl.BlockSpec(memory_space=pltpu.HBM),
        ],
        out_specs=[pl.BlockSpec(memory_space=pltpu.VMEM)] * 2,
        scratch_shapes=[
            pltpu.VMEM((4, step, columns), jnp.float32),
            pltpu.SemaphoreType.DMA((4,)),
        ],
        compiler_params=pltpu.CompilerParams(vmem_limit_bytes=8 * 1024 * 1024),
        cost_estimate=pl.CostEstimate(
            flops=0, bytes_accessed=covariance.size * 4, transcendentals=0
        ),
    )(shift, pltpu.with_memory_space_constraint(covariance, pltpu.HBM))


def slot_kernel(first_k, parts, places, block, high, low, *rest):
    others, outs = rest[:parts], rest[parts:]
    rows, depth = block.shape
    columns = high.shape[1]
    step = math.gcd(depth, 4096)
    total = jnp.zeros((rows, columns), jnp.float32)
    for k in range(0, depth, step):
        values = block[:, k : k + step]
        upper = jnp.clip(values, -largest_bf16, largest_bf16).astype(jnp.bfloat16)
        lower = (values - upper.astype(jnp.float32)).astype(jnp.bfloat16)
        both = jnp.concatenate([upper, lower], 0)
        span = slice(first_k + k, first_k + k + step)
        main = jnp.dot(both, high[span], preferred_element_type=jnp.float32)
        cross = jnp.dot(upper, low[span], preferred_element_type=jnp.float32)
        total += main[:rows] + main[rows:] + cross
    if first_k == 0:
        current = block[:, pl.ds(pl.multiple_of(places[0], columns), columns)]
        row_ids = lax.broadcasted_iota(jnp.int32, (rows, columns), 0) + places[1]
        mask = row_ids == lax.broadcasted_iota(jnp.int32, (rows, columns), 1)
        total += jnp.where(mask, step_size / jnp.where(mask, current, 1.0), 0.0)
    if not parts:
        outs[0][...] = total
        return
    values = [part[...] for part in others]
    values[-1] += total
    per_share = outs[0].shape[0] // rows
    for share, out in enumerate(outs):
        for b in range(per_share):
            found = jnp.zeros((rows, columns), jnp.float32)
            for part, value in enumerate(values):
                found = jnp.where(places[2 + part] == share * per_share + b, value, found)
            out[b * rows : (b + 1) * rows] = found


def slot_product(places, block, weights, first_k=0, others=(), shares=1):
    rows, columns = block.shape[0], weights[0].shape[1]
    shape = (rows * max(len(others), 1) // shares, columns)
    return pl.pallas_call(
        functools.partial(slot_kernel, first_k, len(others)),
        out_shape=[jax.ShapeDtypeStruct(shape, jnp.float32)] * shares,
        in_specs=[pl.BlockSpec(memory_space=pltpu.SMEM)]
        + [pl.BlockSpec(memory_space=pltpu.VMEM)] * (3 + len(others)),
        out_specs=[pl.BlockSpec(memory_space=pltpu.VMEM)] * shares,
        compiler_params=pltpu.CompilerParams(vmem_limit_bytes=(2 + len(others) // 4) * 1024 * 1024),
        cost_estimate=pl.CostEstimate(flops=0, bytes_accessed=block.size * 4, transcendentals=0),
    )(places, block, *[pltpu.with_memory_space_constraint(w, pltpu.VMEM) for w in weights], *others)


def sum_of(terms):
    total = terms[0]
    for term in terms[1:]:
        total = total + term
    return total


def per_device(omega_rows, covariance_columns, tile_offsets):
    team_count = lax.axis_size("team")
    rep_count = lax.axis_size("rep")
    team_index = lax.axis_index("team")
    rep_index = lax.axis_index("rep")
    block_rows, part_width = omega_rows.shape
    tile_width = covariance_columns.shape[1]
    all_rows = block_rows * team_count
    rows_share = all_rows // rep_count
    offset = tile_offsets[0]
    assert all_rows <= part_width and part_width % tile_width == 0
    assert rows_share % block_rows == 0

    shift = jnp.reshape(offset - rep_index * part_width, (1,)).astype(jnp.int32)
    weights = weights_of(covariance_columns, shift)

    half = part_width // 2
    assert all_rows <= half and half % tile_width == 0

    def places_of(source, *more):
        start = jnp.clip(offset, 0, half - tile_width)
        shift = jnp.where(rep_index == 0, source * block_rows - offset, 1 << 20)
        return jnp.stack([start, shift, *more]).astype(jnp.int32)

    ring = list(range(0, team_count, 2)) + list(range(1, team_count, 2))[::-1]
    onward = [(ring[k], ring[(k + 1) % team_count]) for k in range(team_count)]
    backward = [(to, source) for source, to in onward]
    rank = team_index // 2
    place = jnp.where(team_index % 2 == 0, rank, team_count - 1 - rank)

    def device_at(spot):
        spot = spot % team_count
        up = 2 * spot
        return jnp.where(up < team_count, up, 2 * team_count - 1 - up)

    first = lax.ppermute(omega_rows, "team", onward)
    own_part = slot_product(places_of(team_index), omega_rows, weights)
    own, *own_part = lax.optimization_barrier((omega_rows, *own_part))
    last_step = team_count // 2
    gathered = [(first, 1)]
    held = first
    for step in range(2, last_step):
        held = lax.ppermute(held, "team", onward)
        gathered.append((held, step))
    last_held = held
    held = own
    for step in range(1, team_count - last_step):
        held = lax.ppermute(held, "team", backward)
        gathered.append((held, -step))

    last_left = lax.ppermute(last_held[:, :half], "team", onward)
    others, sources = own_part, [team_index]
    for block, step in gathered:
        source = device_at(place - step)
        others += slot_product(places_of(source), block, weights)
        sources.append(source)
        if step == 1:
            last_held, others[-1] = lax.optimization_barrier((last_held, others[-1]))
    last_right = lax.ppermute(last_held[:, half:], "team", onward)
    source = device_at(place - last_step)
    others += slot_product(places_of(source), last_left, weights)
    sources.append(source)

    share_blocks = rows_share // block_rows
    spots = [(source - rep_index * share_blocks) % team_count for source in sources]
    shares = slot_product(
        places_of(source, *spots), last_right, weights, half, others, rep_count
    )
    terms = [shares[0]]
    for by in range(1, rep_count):
        pairs = [(d, (d + by) % rep_count) for d in range(rep_count)]
        terms.append(lax.ppermute(shares[by], "rep", pairs))
    moved = sum_of(terms)

    global_rows = rep_index * rows_share + jnp.arange(rows_share, dtype=jnp.int32)
    global_cols = offset + jnp.arange(tile_width, dtype=jnp.int32)
    diagonal = global_rows[:, None] == global_cols[None, :]
    shrunk = jnp.sign(moved) * jnp.maximum(jnp.abs(moved) - step_size * penalty, 0.0)
    return jnp.where(diagonal, moved, shrunk)


def solution(mesh):
    in_specs = (P(("groups", "team"), "rep"), P("rep", ("groups", "team")), P(("groups", "team")))
    out_specs = P("rep", ("groups", "team"))
    return jax.shard_map(
        per_device, mesh=mesh, in_specs=in_specs, out_specs=out_specs, check_vma=False
    )
```

```python
import functools
import math

import jax
import jax.numpy as jnp
from jax import lax
from jax.experimental import pallas as pl
from jax.experimental.pallas import tpu as pltpu
from jax.sharding import PartitionSpec as P

step_size = 0.5
penalty = 0.1
largest_bf16 = 3.3895313892515355e38


def halves(array):
    high = lax.reduce_precision(jnp.clip(array, -largest_bf16, largest_bf16), 8, 7)
    return high.astype(jnp.bfloat16), (array - high).astype(jnp.bfloat16)


def slots_kernel(first_k, blocks_count, parts_count, places, *refs):
    blocks, refs = refs[:blocks_count], refs[blocks_count:]
    high, low, *refs = refs
    parts, outs = refs[:parts_count], refs[parts_count:]
    rows, depth = blocks[0].shape
    columns = high.shape[1]
    step = math.gcd(depth, 4096)
    all_rows = rows * blocks_count
    total = jnp.zeros((all_rows, columns), jnp.float32)
    for k in range(0, depth, step):
        values = jnp.concatenate([block[:, k : k + step] for block in blocks], 0)
        upper = jnp.clip(values, -largest_bf16, largest_bf16).astype(jnp.bfloat16)
        lower = (values - upper.astype(jnp.float32)).astype(jnp.bfloat16)
        both = jnp.concatenate([upper, lower], 0)
        span = slice(first_k + k, first_k + k + step)
        main = jnp.dot(both, high[span], preferred_element_type=jnp.float32)
        cross = jnp.dot(upper, low[span], preferred_element_type=jnp.float32)
        total += main[:all_rows] + main[all_rows:] + cross
    totals = [total[b * rows : (b + 1) * rows] for b in range(blocks_count)]
    if first_k == 0:
        start = pl.multiple_of(places[0], columns)
        ahead = lax.broadcasted_iota(jnp.int32, (rows, columns), 1)
        ahead -= lax.broadcasted_iota(jnp.int32, (rows, columns), 0)
        for b, block in enumerate(blocks):
            current = block[:, pl.ds(start, columns)]
            mask = ahead == places[1 + b]
            inverse = step_size / jnp.where(mask, current, 1.0)
            totals[b] += jnp.where(mask, inverse, 0.0)
    if not parts_count:
        for out, value in zip(outs, totals):
            out[...] = value
        return
    values = [part[...] for part in parts]
    values[-1] += totals[0]
    per_out = outs[0].shape[0] // rows
    for o, out in enumerate(outs):
        for b in range(per_out):
            found = jnp.zeros((rows, columns), jnp.float32)
            for part, value in enumerate(values):
                found = jnp.where(places[part] == o * per_out + b, value, found)
            out[b * rows : (b + 1) * rows] = found


def slot_products(places, blocks, weights, first_k=0, parts=()):
    rows, columns = blocks[0].shape[0], weights[0].shape[1]
    outs = 2 if parts else len(blocks)
    shape = (rows * len(parts) // 2 if parts else rows, columns)
    return pl.pallas_call(
        functools.partial(slots_kernel, first_k, len(blocks), len(parts)),
        out_shape=[jax.ShapeDtypeStruct(shape, jnp.float32)] * outs,
        in_specs=[pl.BlockSpec(memory_space=pltpu.SMEM)]
        + [pl.BlockSpec(memory_space=pltpu.VMEM)] * (len(blocks) + 2 + len(parts)),
        out_specs=[pl.BlockSpec(memory_space=pltpu.VMEM)] * outs,
        compiler_params=pltpu.CompilerParams(
            vmem_limit_bytes=(4 + len(parts) // 4) * 1024 * 1024
        ),
        cost_estimate=pl.CostEstimate(
            flops=0, bytes_accessed=blocks[0].size * 4, transcendentals=0
        ),
    )(places, *blocks, *weights, *parts)


def sum_of(terms):
    total = terms[0]
    for term in terms[1:]:
        total = total + term
    return total


def per_device(omega_rows, covariance_columns, tile_offsets):
    team_count = lax.axis_size("team")
    rep_count = lax.axis_size("rep")
    team_index = lax.axis_index("team")
    rep_index = lax.axis_index("rep")
    block_rows, part_width = omega_rows.shape
    tile_width = covariance_columns.shape[1]
    all_rows = block_rows * team_count
    rows_share = all_rows // rep_count
    offset = tile_offsets[0]
    assert all_rows <= part_width and part_width % tile_width == 0
    assert rows_share % block_rows == 0 and rep_count & (rep_count - 1) == 0 and rep_count > 1

    k_ids = rep_index * part_width + jnp.arange(part_width, dtype=jnp.int32)
    c_ids = offset + jnp.arange(tile_width, dtype=jnp.int32)
    chosen = (k_ids[:, None] == c_ids[None, :]).astype(jnp.float32)
    weights = halves(chosen - step_size * covariance_columns)

    half = part_width // 2
    assert all_rows <= half and half % tile_width == 0

    def products_of(blocks, sources):
        start = jnp.clip(offset, 0, half - tile_width)
        shifts = [
            jnp.where(rep_index == 0, source * block_rows - offset, 1 << 20) for source in sources
        ]
        places = jnp.stack([start, *shifts]).astype(jnp.int32)
        return slot_products(places, blocks, weights)

    ring = list(range(0, team_count, 2)) + list(range(1, team_count, 2))[::-1]
    onward = [(ring[k], ring[(k + 1) % team_count]) for k in range(team_count)]
    backward = [(to, source) for source, to in onward]
    rank = team_index // 2
    place = jnp.where(team_index % 2 == 0, rank, team_count - 1 - rank)

    def device_at(spot):
        spot = spot % team_count
        up = 2 * spot
        return jnp.where(up < team_count, up, 2 * team_count - 1 - up)

    first = lax.ppermute(omega_rows, "team", onward)
    own, *weights = lax.optimization_barrier((omega_rows, *weights))
    last_step = team_count // 2
    gathered = []
    held = first
    for step in range(2, last_step):
        held = lax.ppermute(held, "team", onward)
        gathered.append((held, step))
    last_held = held
    held = own
    for step in range(1, team_count - last_step):
        held = lax.ppermute(held, "team", backward)
        gathered.append((held, -step))

    last_left = lax.ppermute(last_held[:, :half], "team", onward)
    sources = [team_index, device_at(place - 1)]
    parts = products_of([own, first], sources)
    last_held, *parts = lax.optimization_barrier((last_held, *parts))
    last_right = lax.ppermute(last_held[:, half:], "team", onward)
    for block, step in gathered:
        sources.append(device_at(place - step))
        parts += products_of([block], sources[-1:])
    sources.append(device_at(place - last_step))
    parts += products_of([last_left], sources[-1:])

    share_blocks = rows_share // block_rows
    spots = [
        ((source // share_blocks) ^ rep_index) * share_blocks + source % share_blocks
        for source in sources
    ]
    kept, sent = slot_products(
        jnp.stack(spots).astype(jnp.int32), [last_right], weights, half, parts
    )
    flip = rep_count // 2
    while True:
        pairs = [(d, d ^ flip) for d in range(rep_count)]
        kept = kept + lax.ppermute(sent, "rep", pairs)
        flip //= 2
        if not flip:
            break
        kept, sent = kept[: flip * rows_share], kept[flip * rows_share :]
    moved = kept

    global_rows = rep_index * rows_share + jnp.arange(rows_share, dtype=jnp.int32)
    global_cols = offset + jnp.arange(tile_width, dtype=jnp.int32)
    diagonal = global_rows[:, None] == global_cols[None, :]
    shrunk = jnp.sign(moved) * jnp.maximum(jnp.abs(moved) - step_size * penalty, 0.0)
    return jnp.where(diagonal, moved, shrunk)


def solution(mesh):
    in_specs = (P(("groups", "team"), "rep"), P("rep", ("groups", "team")), P(("groups", "team")))
    out_specs = P("rep", ("groups", "team"))
    return jax.shard_map(
        per_device, mesh=mesh, in_specs=in_specs, out_specs=out_specs, check_vma=False
    )
```

```python
import functools
import math

import jax
import jax.numpy as jnp
from jax import lax
from jax.experimental import pallas as pl
from jax.experimental.pallas import tpu as pltpu
from jax.sharding import PartitionSpec as P

step_size = 0.5
penalty = 0.1
largest_bf16 = 3.3895313892515355e38


def halves(array):
    high = lax.reduce_precision(jnp.clip(array, -largest_bf16, largest_bf16), 8, 7)
    return high.astype(jnp.bfloat16), (array - high).astype(jnp.bfloat16)


def slots_kernel(first_k, blocks_count, parts_count, places, *refs):
    blocks, refs = refs[:blocks_count], refs[blocks_count:]
    high, low, *refs = refs
    parts, outs = refs[:parts_count], refs[parts_count:]
    rows, depth = blocks[0].shape
    columns = high.shape[1]
    step = math.gcd(depth, 4096)
    all_rows = rows * blocks_count
    total = jnp.zeros((all_rows, columns), jnp.float32)
    for k in range(0, depth, step):
        values = jnp.concatenate([block[:, k : k + step] for block in blocks], 0)
        upper = jnp.clip(values, -largest_bf16, largest_bf16).astype(jnp.bfloat16)
        lower = (values - upper.astype(jnp.float32)).astype(jnp.bfloat16)
        both = jnp.concatenate([upper, lower], 0)
        span = slice(first_k + k, first_k + k + step)
        main = jnp.dot(both, high[span], preferred_element_type=jnp.float32)
        cross = jnp.dot(upper, low[span], preferred_element_type=jnp.float32)
        total += main[:all_rows] + main[all_rows:] + cross
    totals = [total[b * rows : (b + 1) * rows] for b in range(blocks_count)]
    if first_k == 0:
        start = pl.multiple_of(places[0], columns)
        ahead = lax.broadcasted_iota(jnp.int32, (rows, columns), 1)
        ahead -= lax.broadcasted_iota(jnp.int32, (rows, columns), 0)
        for b, block in enumerate(blocks):
            current = block[:, pl.ds(start, columns)]
            mask = ahead == places[1 + b]
            inverse = step_size / jnp.where(mask, current, 1.0)
            totals[b] += jnp.where(mask, inverse, 0.0)
    if not parts_count:
        for out, value in zip(outs, totals):
            out[...] = value
        return
    values = [part[...] for part in parts]
    values[-1] += totals[0]
    per_out = outs[0].shape[0] // rows
    for o, out in enumerate(outs):
        for b in range(per_out):
            found = jnp.zeros((rows, columns), jnp.float32)
            for part, value in enumerate(values):
                found = jnp.where(places[part] == o * per_out + b, value, found)
            out[b * rows : (b + 1) * rows] = found


def slot_products(places, blocks, weights, first_k=0, parts=(), shares=0):
    rows, columns = blocks[0].shape[0], weights[0].shape[1]
    outs = shares or len(blocks)
    shape = (rows * len(parts) // shares if shares else rows, columns)
    return pl.pallas_call(
        functools.partial(slots_kernel, first_k, len(blocks), len(parts)),
        out_shape=[jax.ShapeDtypeStruct(shape, jnp.float32)] * outs,
        in_specs=[pl.BlockSpec(memory_space=pltpu.SMEM)]
        + [pl.BlockSpec(memory_space=pltpu.VMEM)] * (len(blocks) + 2 + len(parts)),
        out_specs=[pl.BlockSpec(memory_space=pltpu.VMEM)] * outs,
        compiler_params=pltpu.CompilerParams(
            vmem_limit_bytes=(4 + len(parts) // 4) * 1024 * 1024
        ),
        cost_estimate=pl.CostEstimate(
            flops=0, bytes_accessed=blocks[0].size * 4, transcendentals=0
        ),
    )(places, *blocks, *weights, *parts)


def sum_of(terms):
    total = terms[0]
    for term in terms[1:]:
        total = total + term
    return total


def per_device(omega_rows, covariance_columns, tile_offsets):
    team_count = lax.axis_size("team")
    rep_count = lax.axis_size("rep")
    team_index = lax.axis_index("team")
    rep_index = lax.axis_index("rep")
    block_rows, part_width = omega_rows.shape
    tile_width = covariance_columns.shape[1]
    all_rows = block_rows * team_count
    rows_share = all_rows // rep_count
    offset = tile_offsets[0]
    assert all_rows <= part_width and part_width % tile_width == 0
    assert rows_share % block_rows == 0 and rep_count & (rep_count - 1) == 0 and rep_count > 1

    k_ids = rep_index * part_width + jnp.arange(part_width, dtype=jnp.int32)
    c_ids = offset + jnp.arange(tile_width, dtype=jnp.int32)
    chosen = (k_ids[:, None] == c_ids[None, :]).astype(jnp.float32)
    weights = halves(chosen - step_size * covariance_columns)

    half = part_width // 2
    assert all_rows <= half and half % tile_width == 0

    def products_of(blocks, sources):
        start = jnp.clip(offset, 0, half - tile_width)
        shifts = [
            jnp.where(rep_index == 0, source * block_rows - offset, 1 << 20) for source in sources
        ]
        places = jnp.stack([start, *shifts]).astype(jnp.int32)
        return slot_products(places, blocks, weights)

    ring = list(range(0, team_count, 2)) + list(range(1, team_count, 2))[::-1]
    onward = [(ring[k], ring[(k + 1) % team_count]) for k in range(team_count)]
    backward = [(to, source) for source, to in onward]
    rank = team_index // 2
    place = jnp.where(team_index % 2 == 0, rank, team_count - 1 - rank)

    def device_at(spot):
        spot = spot % team_count
        up = 2 * spot
        return jnp.where(up < team_count, up, 2 * team_count - 1 - up)

    first = lax.ppermute(omega_rows, "team", onward)
    own, *weights = lax.optimization_barrier((omega_rows, *weights))
    last_step = team_count // 2
    gathered = []
    held = first
    for step in range(2, last_step):
        held = lax.ppermute(held, "team", onward)
        gathered.append((held, step))
    last_held = held
    held = own
    for step in range(1, team_count - last_step):
        held = lax.ppermute(held, "team", backward)
        gathered.append((held, -step))

    last_left = lax.ppermute(last_held[:, :half], "team", onward)
    sources = [team_index, device_at(place - 1)]
    parts = products_of([own, first], sources)
    last_held, *parts = lax.optimization_barrier((last_held, *parts))
    last_right = lax.ppermute(last_held[:, half:], "team", onward)
    for block, step in gathered:
        sources.append(device_at(place - step))
        parts += products_of([block], sources[-1:])
    sources.append(device_at(place - last_step))
    parts += products_of([last_left], sources[-1:])

    share_blocks = rows_share // block_rows
    spots = [
        ((source // share_blocks) ^ rep_index) * share_blocks + source % share_blocks
        for source in sources
    ]
    shares = slot_products(
        jnp.stack(spots).astype(jnp.int32), [last_right], weights, half, parts, rep_count
    )
    terms = [shares[0]]
    for flip in range(rep_count - 1, 0, -1):
        pairs = [(d, d ^ flip) for d in range(rep_count)]
        terms.append(lax.ppermute(shares[flip], "rep", pairs))
    moved = sum_of(terms)

    global_rows = rep_index * rows_share + jnp.arange(rows_share, dtype=jnp.int32)
    global_cols = offset + jnp.arange(tile_width, dtype=jnp.int32)
    diagonal = global_rows[:, None] == global_cols[None, :]
    shrunk = jnp.sign(moved) * jnp.maximum(jnp.abs(moved) - step_size * penalty, 0.0)
    return jnp.where(diagonal, moved, shrunk)


def solution(mesh):
    in_specs = (P(("groups", "team"), "rep"), P("rep", ("groups", "team")), P(("groups", "team")))
    out_specs = P("rep", ("groups", "team"))
    return jax.shard_map(
        per_device, mesh=mesh, in_specs=in_specs, out_specs=out_specs, check_vma=False
    )
```

```python
import functools
import math

import jax
import jax.numpy as jnp
from jax import lax
from jax.experimental import pallas as pl
from jax.experimental.pallas import tpu as pltpu
from jax.sharding import PartitionSpec as P

step_size = 0.5
penalty = 0.1
largest_bf16 = 3.3895313892515355e38


def halves(array):
    high = lax.reduce_precision(jnp.clip(array, -largest_bf16, largest_bf16), 8, 7)
    return high.astype(jnp.bfloat16), (array - high).astype(jnp.bfloat16)


def slots_kernel(first_k, blocks_count, parts_count, places, *refs):
    blocks, refs = refs[:blocks_count], refs[blocks_count:]
    high, low, *refs = refs
    parts, outs = refs[:parts_count], refs[parts_count:]
    rows, depth = blocks[0].shape
    columns = high.shape[1]
    step = math.gcd(depth, 2048)
    all_rows = rows * blocks_count
    total = jnp.zeros((all_rows, columns), jnp.float32)
    for k in range(0, depth, step):
        values = jnp.concatenate([block[:, k : k + step] for block in blocks], 0)
        upper = jnp.clip(values, -largest_bf16, largest_bf16).astype(jnp.bfloat16)
        lower = (values - upper.astype(jnp.float32)).astype(jnp.bfloat16)
        both = jnp.concatenate([upper, lower], 0)
        span = slice(first_k + k, first_k + k + step)
        main = jnp.dot(both, high[span], preferred_element_type=jnp.float32)
        cross = jnp.dot(upper, low[span], preferred_element_type=jnp.float32)
        total += main[:all_rows] + main[all_rows:] + cross
    totals = [total[b * rows : (b + 1) * rows] for b in range(blocks_count)]
    if first_k == 0:
        start = pl.multiple_of(places[0], columns)
        ahead = lax.broadcasted_iota(jnp.int32, (rows, columns), 1)
        ahead -= lax.broadcasted_iota(jnp.int32, (rows, columns), 0)
        for b, block in enumerate(blocks):
            current = block[:, pl.ds(start, columns)]
            mask = ahead == places[1 + b]
            inverse = step_size / jnp.where(mask, current, 1.0)
            totals[b] += jnp.where(mask, inverse, 0.0)
    if not parts_count:
        for out, value in zip(outs, totals):
            out[...] = value
        return
    values = [part[...] for part in parts]
    values[-1] += totals[0]
    per_out = outs[0].shape[0] // rows
    for o, out in enumerate(outs):
        for b in range(per_out):
            found = jnp.zeros((rows, columns), jnp.float32)
            for part, value in enumerate(values):
                found = jnp.where(places[part] == o * per_out + b, value, found)
            out[b * rows : (b + 1) * rows] = found


def slot_products(places, blocks, weights, first_k=0, parts=(), shares=0):
    rows, columns = blocks[0].shape[0], weights[0].shape[1]
    outs = shares or len(blocks)
    shape = (rows * len(parts) // shares if shares else rows, columns)
    return pl.pallas_call(
        functools.partial(slots_kernel, first_k, len(blocks), len(parts)),
        out_shape=[jax.ShapeDtypeStruct(shape, jnp.float32)] * outs,
        in_specs=[pl.BlockSpec(memory_space=pltpu.SMEM)]
        + [pl.BlockSpec(memory_space=pltpu.VMEM)] * (len(blocks) + 2 + len(parts)),
        out_specs=[pl.BlockSpec(memory_space=pltpu.VMEM)] * outs,
        compiler_params=pltpu.CompilerParams(
            vmem_limit_bytes=(4 + len(parts) // 4) * 1024 * 1024
        ),
        cost_estimate=pl.CostEstimate(
            flops=0, bytes_accessed=blocks[0].size * 4, transcendentals=0
        ),
    )(places, *blocks, *weights, *parts)


def sum_of(terms):
    total = terms[0]
    for term in terms[1:]:
        total = total + term
    return total


def per_device(omega_rows, covariance_columns, tile_offsets):
    team_count = lax.axis_size("team")
    rep_count = lax.axis_size("rep")
    team_index = lax.axis_index("team")
    rep_index = lax.axis_index("rep")
    block_rows, part_width = omega_rows.shape
    tile_width = covariance_columns.shape[1]
    all_rows = block_rows * team_count
    rows_share = all_rows // rep_count
    offset = tile_offsets[0]
    assert all_rows <= part_width and part_width % tile_width == 0
    assert rows_share % block_rows == 0 and rep_count & (rep_count - 1) == 0 and rep_count > 1

    k_ids = rep_index * part_width + jnp.arange(part_width, dtype=jnp.int32)
    c_ids = offset + jnp.arange(tile_width, dtype=jnp.int32)
    chosen = (k_ids[:, None] == c_ids[None, :]).astype(jnp.float32)
    weights = halves(chosen - step_size * covariance_columns)

    cut = part_width // 4 * 3
    assert all_rows <= cut and cut % tile_width == 0

    def products_of(blocks, sources):
        start = jnp.clip(offset, 0, cut - tile_width)
        shifts = [
            jnp.where(rep_index == 0, source * block_rows - offset, 1 << 20) for source in sources
        ]
        places = jnp.stack([start, *shifts]).astype(jnp.int32)
        return slot_products(places, blocks, weights)

    ring = list(range(0, team_count, 2)) + list(range(1, team_count, 2))[::-1]
    onward = [(ring[k], ring[(k + 1) % team_count]) for k in range(team_count)]
    backward = [(to, source) for source, to in onward]
    rank = team_index // 2
    place = jnp.where(team_index % 2 == 0, rank, team_count - 1 - rank)

    def device_at(spot):
        spot = spot % team_count
        up = 2 * spot
        return jnp.where(up < team_count, up, 2 * team_count - 1 - up)

    first = lax.ppermute(omega_rows, "team", onward)
    own, *weights = lax.optimization_barrier((omega_rows, *weights))
    last_step = team_count // 2
    gathered = []
    held = first
    for step in range(2, last_step):
        held = lax.ppermute(held, "team", onward)
        gathered.append((held, step))
    last_held = held
    held = own
    for step in range(1, team_count - last_step):
        held = lax.ppermute(held, "team", backward)
        gathered.append((held, -step))

    last_left = lax.ppermute(last_held[:, :cut], "team", onward)
    sources = [team_index, device_at(place - 1)]
    parts = products_of([own, first], sources)
    last_held, *parts = lax.optimization_barrier((last_held, *parts))
    last_right = lax.ppermute(last_held[:, cut:], "team", onward)
    for block, step in gathered:
        sources.append(device_at(place - step))
        parts += products_of([block], sources[-1:])
    sources.append(device_at(place - last_step))
    parts += products_of([last_left], sources[-1:])

    share_blocks = rows_share // block_rows
    spots = [
        ((source // share_blocks) ^ rep_index) * share_blocks + source % share_blocks
        for source in sources
    ]
    shares = slot_products(
        jnp.stack(spots).astype(jnp.int32), [last_right], weights, cut, parts, rep_count
    )
    terms = [shares[0]]
    for flip in range(rep_count - 1, 0, -1):
        pairs = [(d, d ^ flip) for d in range(rep_count)]
        terms.append(lax.ppermute(shares[flip], "rep", pairs))
    moved = sum_of(terms)

    global_rows = rep_index * rows_share + jnp.arange(rows_share, dtype=jnp.int32)
    global_cols = offset + jnp.arange(tile_width, dtype=jnp.int32)
    diagonal = global_rows[:, None] == global_cols[None, :]
    shrunk = jnp.sign(moved) * jnp.maximum(jnp.abs(moved) - step_size * penalty, 0.0)
    return jnp.where(diagonal, moved, shrunk)


def solution(mesh):
    in_specs = (P(("groups", "team"), "rep"), P("rep", ("groups", "team")), P(("groups", "team")))
    out_specs = P("rep", ("groups", "team"))
    return jax.shard_map(
        per_device, mesh=mesh, in_specs=in_specs, out_specs=out_specs, check_vma=False
    )
```

```python
import functools
import math

import jax
import jax.numpy as jnp
from jax import lax
from jax.experimental import pallas as pl
from jax.experimental.pallas import tpu as pltpu
from jax.sharding import PartitionSpec as P

step_size = 0.5
penalty = 0.1
largest_bf16 = 3.3895313892515355e38


def halves(array):
    high = lax.reduce_precision(jnp.clip(array, -largest_bf16, largest_bf16), 8, 7)
    return high.astype(jnp.bfloat16), (array - high).astype(jnp.bfloat16)


def slots_kernel(firsts, parts_count, shares, places, *refs):
    blocks, refs = refs[: len(firsts)], refs[len(firsts) :]
    high, low, *refs = refs
    parts, outs = refs[:parts_count], refs[parts_count:]
    rows, columns = blocks[0].shape[0], high.shape[1]
    totals = [None] * len(firsts)
    for first_k in sorted(set(firsts)):
        group = [b for b, first in enumerate(firsts) if first == first_k]
        all_rows = rows * len(group)
        depth = blocks[group[0]].shape[1]
        step = math.gcd(depth, 2048)
        total = jnp.zeros((all_rows, columns), jnp.float32)
        for k in range(0, depth, step):
            values = jnp.concatenate([blocks[b][:, k : k + step] for b in group], 0)
            upper = jnp.clip(values, -largest_bf16, largest_bf16).astype(jnp.bfloat16)
            lower = (values - upper.astype(jnp.float32)).astype(jnp.bfloat16)
            both = jnp.concatenate([upper, lower], 0)
            span = slice(first_k + k, first_k + k + step)
            main = jnp.dot(both, high[span], preferred_element_type=jnp.float32)
            cross = jnp.dot(upper, low[span], preferred_element_type=jnp.float32)
            total += main[:all_rows] + main[all_rows:] + cross
        for position, b in enumerate(group):
            totals[b] = total[position * rows : (position + 1) * rows]
    if 0 in firsts:
        start = pl.multiple_of(places[0], columns)
        ahead = lax.broadcasted_iota(jnp.int32, (rows, columns), 1)
        ahead -= lax.broadcasted_iota(jnp.int32, (rows, columns), 0)
        for b, block in enumerate(blocks):
            if firsts[b] == 0:
                current = block[:, pl.ds(start, columns)]
                mask = ahead == places[1 + b]
                inverse = step_size / jnp.where(mask, current, 1.0)
                totals[b] += jnp.where(mask, inverse, 0.0)
    if not shares:
        for out, value in zip(outs, totals):
            out[...] = value
        return
    values = [part[...] for part in parts] + totals
    per_out = outs[0].shape[0] // rows
    for o, out in enumerate(outs):
        for b in range(per_out):
            found = jnp.zeros((rows, columns), jnp.float32)
            for position, value in enumerate(values):
                mine = places[1 + len(firsts) + position] == o * per_out + b
                found += jnp.where(mine, value, 0.0)
            out[b * rows : (b + 1) * rows] = found


def slot_products(places, blocks, firsts, weights, parts=(), shares=0, per_share=1):
    rows, columns = blocks[0].shape[0], weights[0].shape[1]
    outs = shares or len(blocks)
    shape = (rows * per_share if shares else rows, columns)
    return pl.pallas_call(
        functools.partial(slots_kernel, tuple(firsts), len(parts), shares),
        out_shape=[jax.ShapeDtypeStruct(shape, jnp.float32)] * outs,
        in_specs=[pl.BlockSpec(memory_space=pltpu.SMEM)]
        + [pl.BlockSpec(memory_space=pltpu.VMEM)] * (len(blocks) + 2 + len(parts)),
        out_specs=[pl.BlockSpec(memory_space=pltpu.VMEM)] * outs,
        compiler_params=pltpu.CompilerParams(
            vmem_limit_bytes=(4 + len(parts) // 4) * 1024 * 1024
        ),
        cost_estimate=pl.CostEstimate(
            flops=0, bytes_accessed=blocks[0].size * 4, transcendentals=0
        ),
    )(places, *blocks, *weights, *parts)


def sum_of(terms):
    total = terms[0]
    for term in terms[1:]:
        total = total + term
    return total


def per_device(omega_rows, covariance_columns, tile_offsets):
    team_count = lax.axis_size("team")
    rep_count = lax.axis_size("rep")
    team_index = lax.axis_index("team")
    rep_index = lax.axis_index("rep")
    block_rows, part_width = omega_rows.shape
    tile_width = covariance_columns.shape[1]
    all_rows = block_rows * team_count
    rows_share = all_rows // rep_count
    offset = tile_offsets[0]
    assert all_rows <= part_width and part_width % tile_width == 0
    assert rows_share % block_rows == 0 and rep_count & (rep_count - 1) == 0 and rep_count > 1

    k_ids = rep_index * part_width + jnp.arange(part_width, dtype=jnp.int32)
    c_ids = offset + jnp.arange(tile_width, dtype=jnp.int32)
    chosen = (k_ids[:, None] == c_ids[None, :]).astype(jnp.float32)
    weights = halves(chosen - step_size * covariance_columns)

    cut = part_width // 4 * 3
    assert all_rows <= cut and cut % tile_width == 0
    share_blocks = rows_share // block_rows

    def products_of(blocks, sources, firsts=None, spots=(), parts=(), shares=0):
        start = jnp.clip(offset, 0, cut - tile_width)
        shifts = [
            jnp.where(rep_index == 0, source * block_rows - offset, 1 << 20) for source in sources
        ]
        places = jnp.stack([start, *shifts, *spots]).astype(jnp.int32)
        firsts = firsts or [0] * len(blocks)
        return slot_products(places, blocks, firsts, weights, parts, shares, share_blocks)

    def spots_of(sources):
        return [
            ((source // share_blocks) ^ rep_index) * share_blocks + source % share_blocks
            for source in sources
        ]

    def exchanged(share, flip):
        pairs = [(d, d ^ flip) for d in range(rep_count)]
        return lax.ppermute(share, "rep", pairs)

    ring = list(range(0, team_count, 2)) + list(range(1, team_count, 2))[::-1]
    onward = [(ring[k], ring[(k + 1) % team_count]) for k in range(team_count)]
    backward = [(to, source) for source, to in onward]
    rank = team_index // 2
    place = jnp.where(team_index % 2 == 0, rank, team_count - 1 - rank)

    def device_at(spot):
        spot = spot % team_count
        up = 2 * spot
        return jnp.where(up < team_count, up, 2 * team_count - 1 - up)

    if team_count == 4 and rep_count == 4:
        own_left, own_right = omega_rows[:, :cut], omega_rows[:, cut:]
        two_apart = [(0, 2), (1, 3), (2, 0), (3, 1)]
        neighbours = [(0, 1), (1, 0), (2, 3), (3, 2)]
        home = team_index // 2 == rep_index // 2
        left1 = lax.ppermute(own_left, "team", onward)
        own_left, own_right, *weights = lax.optimization_barrier((own_left, own_right, *weights))
        right1 = lax.ppermute(own_right, "team", two_apart)
        left2 = lax.ppermute(own_left, "team", backward)
        left3 = lax.ppermute(left1, "team", onward)
        sources = [team_index, device_at(place - 1), team_index, team_index ^ 2]
        early = jnp.where(home, right1, own_right)
        late = jnp.where(home, own_right, right1)
        right2 = lax.ppermute(early, "team", neighbours)
        parts = products_of([own_left, left1, own_right, right1], sources, [0, 0, cut, cut])
        sources.append(device_at(place + 1))
        parts += products_of([left2], sources[-1:])
        late, *parts = lax.optimization_barrier((late, *parts))
        right3 = lax.ppermute(late, "team", neighbours)
        sources += [device_at(place - 2), jnp.where(home, team_index ^ 3, team_index ^ 1)]
        shares = products_of([left3, right2], sources[-2:], [0, cut], spots_of(sources), parts, 4)
        terms = [exchanged(shares[flip], flip) for flip in (3, 2)]
        source = jnp.where(home, team_index ^ 1, team_index ^ 3)
        kept, for_mate = products_of(
            [right3], [source], [cut], [0, 1] + spots_of([source]), shares[:2], 2
        )
        for_mate, *terms = lax.optimization_barrier((for_mate, *terms))
        moved = sum_of([kept, *terms, exchanged(for_mate, 1)])
    else:
        first = lax.ppermute(omega_rows, "team", onward)
        own, *weights = lax.optimization_barrier((omega_rows, *weights))
        last_step = team_count // 2
        gathered = []
        held = first
        for step in range(2, last_step):
            held = lax.ppermute(held, "team", onward)
            gathered.append((held, step))
        last_held = held
        held = own
        for step in range(1, team_count - last_step):
            held = lax.ppermute(held, "team", backward)
            gathered.append((held, -step))
        last = lax.ppermute(last_held, "team", onward)
        sources = [team_index, device_at(place - 1)]
        parts = products_of([own, first], sources)
        for block, step in gathered:
            sources.append(device_at(place - step))
            parts += products_of([block], sources[-1:])
        sources.append(device_at(place - last_step))
        shares = products_of(
            [last], sources[-1:], None, spots_of(sources), parts, rep_count
        )
        moved = sum_of([shares[0]] + [exchanged(shares[s], s) for s in range(1, rep_count)])

    global_rows = rep_index * rows_share + jnp.arange(rows_share, dtype=jnp.int32)
    global_cols = offset + jnp.arange(tile_width, dtype=jnp.int32)
    diagonal = global_rows[:, None] == global_cols[None, :]
    shrunk = jnp.sign(moved) * jnp.maximum(jnp.abs(moved) - step_size * penalty, 0.0)
    return jnp.where(diagonal, moved, shrunk)


def solution(mesh):
    in_specs = (P(("groups", "team"), "rep"), P("rep", ("groups", "team")), P(("groups", "team")))
    out_specs = P("rep", ("groups", "team"))
    return jax.shard_map(
        per_device, mesh=mesh, in_specs=in_specs, out_specs=out_specs, check_vma=False
    )
```

```python
import functools

import jax
import jax.numpy as jnp
from jax import lax
from jax.experimental import pallas as pl
from jax.experimental.pallas import tpu as pltpu
from jax.sharding import PartitionSpec as P

step_size = 0.5
penalty = 0.1
largest_bf16 = 3.3895313892515355e38


def halves(array):
    high = lax.reduce_precision(jnp.clip(array, -largest_bf16, largest_bf16), 8, 7)
    return high.astype(jnp.bfloat16), (array - high).astype(jnp.bfloat16)


def slots_kernel(first_k, blocks_count, parts_count, placed, places, *refs):
    blocks, refs = refs[:blocks_count], refs[blocks_count:]
    high, low, *refs = refs
    parts, outs = refs[:parts_count], refs[parts_count:]
    rows, depth = blocks[0].shape
    columns = high.shape[1]
    pieces = -(-depth // 2048)
    step = depth // pieces
    assert depth % pieces == 0 and step % 128 == 0
    all_rows = rows * blocks_count
    total = jnp.zeros((all_rows, columns), jnp.float32)
    for k in range(0, depth, step):
        values = jnp.concatenate([block[:, k : k + step] for block in blocks], 0)
        upper = jnp.clip(values, -largest_bf16, largest_bf16).astype(jnp.bfloat16)
        lower = (values - upper.astype(jnp.float32)).astype(jnp.bfloat16)
        both = jnp.concatenate([upper, lower], 0)
        span = slice(first_k + k, first_k + k + step)
        main = jnp.dot(both, high[span], preferred_element_type=jnp.float32)
        cross = jnp.dot(upper, low[span], preferred_element_type=jnp.float32)
        total += main[:all_rows] + main[all_rows:] + cross
    totals = [total[b * rows : (b + 1) * rows] for b in range(blocks_count)]
    if first_k == 0:
        start = pl.multiple_of(places[0], columns)
        ahead = lax.broadcasted_iota(jnp.int32, (rows, columns), 1)
        ahead -= lax.broadcasted_iota(jnp.int32, (rows, columns), 0)
        for b, block in enumerate(blocks):
            current = block[:, pl.ds(start, columns)]
            mask = ahead == places[1 + b]
            inverse = step_size / jnp.where(mask, current, 1.0)
            totals[b] += jnp.where(mask, inverse, 0.0)
    if len(outs) == blocks_count:
        for out, value in zip(outs, totals):
            out[...] = value
        return
    per_out = outs[0].shape[0] // rows
    values = [totals[0]] if placed else [part[...] for part in parts] + totals
    spots = 1 if placed else 1 + blocks_count
    for o, out in enumerate(outs):
        for b in range(per_out):
            span = slice(b * rows, (b + 1) * rows)
            found = parts[o][span] if placed else jnp.zeros((rows, columns), jnp.float32)
            for position, value in enumerate(values):
                mine = places[spots + position] == o * per_out + b
                found = found + jnp.where(mine, value, 0.0)
            out[span] = found


def slot_products(places, blocks, weights, first_k=0, parts=(), shares=0, per_share=1):
    rows, columns = blocks[0].shape[0], weights[0].shape[1]
    outs = shares or len(blocks)
    placed = first_k > 0
    shape = (rows * per_share, columns)
    return pl.pallas_call(
        functools.partial(slots_kernel, first_k, len(blocks), len(parts), placed),
        out_shape=[jax.ShapeDtypeStruct(shape, jnp.float32)] * outs,
        in_specs=[pl.BlockSpec(memory_space=pltpu.SMEM)]
        + [pl.BlockSpec(memory_space=pltpu.VMEM)] * (len(blocks) + 2 + len(parts)),
        out_specs=[pl.BlockSpec(memory_space=pltpu.VMEM)] * outs,
        compiler_params=pltpu.CompilerParams(
            vmem_limit_bytes=(4 + len(parts) // 4) * 1024 * 1024
        ),
        cost_estimate=pl.CostEstimate(
            flops=0, bytes_accessed=blocks[0].size * 4, transcendentals=0
        ),
    )(places, *blocks, *weights, *parts)


def sum_of(terms):
    total = terms[0]
    for term in terms[1:]:
        total = total + term
    return total


def per_device(omega_rows, covariance_columns, tile_offsets):
    team_count = lax.axis_size("team")
    rep_count = lax.axis_size("rep")
    team_index = lax.axis_index("team")
    rep_index = lax.axis_index("rep")
    block_rows, part_width = omega_rows.shape
    tile_width = covariance_columns.shape[1]
    all_rows = block_rows * team_count
    rows_share = all_rows // rep_count
    offset = tile_offsets[0]
    assert all_rows <= part_width and part_width % tile_width == 0
    assert rows_share % block_rows == 0 and rep_count & (rep_count - 1) == 0 and rep_count > 1

    k_ids = rep_index * part_width + jnp.arange(part_width, dtype=jnp.int32)
    c_ids = offset + jnp.arange(tile_width, dtype=jnp.int32)
    chosen = (k_ids[:, None] == c_ids[None, :]).astype(jnp.float32)
    weights = halves(chosen - step_size * covariance_columns)

    cut = part_width // 16 * 13
    assert all_rows <= cut and cut % tile_width == 0

    share_blocks = rows_share // block_rows

    def products_of(blocks, sources, spots=(), parts=()):
        start = jnp.clip(offset, 0, cut - tile_width)
        shifts = [
            jnp.where(rep_index == 0, source * block_rows - offset, 1 << 20) for source in sources
        ]
        places = jnp.stack([start, *shifts, *spots]).astype(jnp.int32)
        if not spots:
            return slot_products(places, blocks, weights)
        return slot_products(places, blocks, weights, 0, parts, rep_count, share_blocks)

    ring = list(range(0, team_count, 2)) + list(range(1, team_count, 2))[::-1]
    onward = [(ring[k], ring[(k + 1) % team_count]) for k in range(team_count)]
    backward = [(to, source) for source, to in onward]
    rank = team_index // 2
    place = jnp.where(team_index % 2 == 0, rank, team_count - 1 - rank)

    def device_at(spot):
        spot = spot % team_count
        up = 2 * spot
        return jnp.where(up < team_count, up, 2 * team_count - 1 - up)

    first = lax.ppermute(omega_rows, "team", onward)
    own, *weights = lax.optimization_barrier((omega_rows, *weights))
    last_step = team_count // 2
    gathered = []
    held = first
    for step in range(2, last_step):
        held = lax.ppermute(held, "team", onward)
        gathered.append((held, step))
    last_held = held
    held = own
    for step in range(1, team_count - last_step):
        held = lax.ppermute(held, "team", backward)
        gathered.append((held, -step))

    last_left = lax.ppermute(last_held[:, :cut], "team", onward)
    sources = [team_index, device_at(place - 1)]
    parts = products_of([own, first], sources)
    last_held, *parts = lax.optimization_barrier((last_held, *parts))
    last_right = lax.ppermute(last_held[:, cut:], "team", onward)
    for block, step in gathered:
        sources.append(device_at(place - step))
        parts += products_of([block], sources[-1:])
    sources.append(device_at(place - last_step))

    spots = [
        ((source // share_blocks) ^ rep_index) * share_blocks + source % share_blocks
        for source in sources
    ]
    shares = products_of([last_left], sources[-1:], spots, parts)
    places = jnp.stack([offset, spots[-1]]).astype(jnp.int32)
    shares = slot_products(
        places, [last_right], weights, cut, shares, rep_count, share_blocks
    )
    terms = [shares[0]]
    for flip in range(rep_count - 1, 0, -1):
        pairs = [(d, d ^ flip) for d in range(rep_count)]
        terms.append(lax.ppermute(shares[flip], "rep", pairs))
    moved = sum_of(terms)

    global_rows = rep_index * rows_share + jnp.arange(rows_share, dtype=jnp.int32)
    global_cols = offset + jnp.arange(tile_width, dtype=jnp.int32)
    diagonal = global_rows[:, None] == global_cols[None, :]
    shrunk = jnp.sign(moved) * jnp.maximum(jnp.abs(moved) - step_size * penalty, 0.0)
    return jnp.where(diagonal, moved, shrunk)


def solution(mesh):
    in_specs = (P(("groups", "team"), "rep"), P("rep", ("groups", "team")), P(("groups", "team")))
    out_specs = P("rep", ("groups", "team"))
    return jax.shard_map(
        per_device, mesh=mesh, in_specs=in_specs, out_specs=out_specs, check_vma=False
    )
```

```python
import functools

import jax
import jax.numpy as jnp
from jax import lax
from jax.experimental import pallas as pl
from jax.experimental.pallas import tpu as pltpu
from jax.sharding import PartitionSpec as P

step_size = 0.5
penalty = 0.1
largest_bf16 = 3.3895313892515355e38


def halves(array):
    high = lax.reduce_precision(jnp.clip(array, -largest_bf16, largest_bf16), 8, 7)
    return high.astype(jnp.bfloat16), (array - high).astype(jnp.bfloat16)


def products(blocks, high, low, first_k=0):
    rows, depth = blocks[0].shape
    pieces = -(-depth // 2048)
    step = depth // pieces
    assert depth % pieces == 0 and step % 128 == 0
    all_rows = rows * len(blocks)
    total = jnp.zeros((all_rows, high.shape[1]), jnp.float32)
    for k in range(0, depth, step):
        values = jnp.concatenate([block[:, k : k + step] for block in blocks], 0)
        upper = jnp.clip(values, -largest_bf16, largest_bf16).astype(jnp.bfloat16)
        lower = (values - upper.astype(jnp.float32)).astype(jnp.bfloat16)
        both = jnp.concatenate([upper, lower], 0)
        span = slice(first_k + k, first_k + k + step)
        main = jnp.dot(both, high[span], preferred_element_type=jnp.float32)
        cross = jnp.dot(upper, low[span], preferred_element_type=jnp.float32)
        total += main[:all_rows] + main[all_rows:] + cross
    return [total[b * rows : (b + 1) * rows] for b in range(len(blocks))]


def slots_kernel(blocks_count, parts_count, places, *refs):
    blocks, refs = refs[:blocks_count], refs[blocks_count:]
    high, low, *refs = refs
    parts, outs = refs[:parts_count], refs[parts_count:]
    rows, columns = blocks[0].shape[0], high.shape[1]
    totals = products(blocks, high, low)
    start = pl.multiple_of(places[0], columns)
    ahead = lax.broadcasted_iota(jnp.int32, (rows, columns), 1)
    ahead -= lax.broadcasted_iota(jnp.int32, (rows, columns), 0)
    for b, block in enumerate(blocks):
        current = block[:, pl.ds(start, columns)]
        mask = ahead == places[1 + b]
        inverse = step_size / jnp.where(mask, current, 1.0)
        totals[b] += jnp.where(mask, inverse, 0.0)
    if len(outs) == blocks_count:
        for out, value in zip(outs, totals):
            out[...] = value
        return
    per_out = outs[0].shape[0] // rows
    for o, out in enumerate(outs):
        for b in range(per_out):
            found = jnp.zeros((rows, columns), jnp.float32)
            for position, value in enumerate([part[...] for part in parts] + totals):
                mine = places[1 + blocks_count + position] == o * per_out + b
                found = found + jnp.where(mine, value, 0.0)
            out[b * rows : (b + 1) * rows] = found


def last_kernel(first_k, masks, block, high, low, *refs):
    shares, outs = refs[: len(refs) // 2], refs[len(refs) // 2 :]
    rows = block.shape[0]
    (total,) = products([block], high, low, first_k)
    for o, out in enumerate(outs):
        for b in range(out.shape[0] // rows):
            span = slice(b * rows, (b + 1) * rows)
            out[span] = shares[o][span] + jnp.where(masks[o, span] != 0, total, 0.0)


def call(kernel, count, shape, scalars, arrays, limit):
    return pl.pallas_call(
        kernel,
        out_shape=[jax.ShapeDtypeStruct(shape, jnp.float32)] * count,
        in_specs=[pl.BlockSpec(memory_space=pltpu.SMEM)] * len(scalars)
        + [pl.BlockSpec(memory_space=pltpu.VMEM)] * len(arrays),
        out_specs=[pl.BlockSpec(memory_space=pltpu.VMEM)] * count,
        compiler_params=pltpu.CompilerParams(vmem_limit_bytes=limit * 1024 * 1024),
        cost_estimate=pl.CostEstimate(
            flops=0, bytes_accessed=count * shape[0] * shape[1] * 4, transcendentals=0
        ),
    )(*scalars, *arrays)


def sum_of(terms):
    total = terms[0]
    for term in terms[1:]:
        total = total + term
    return total


def per_device(omega_rows, covariance_columns, tile_offsets):
    team_count = lax.axis_size("team")
    rep_count = lax.axis_size("rep")
    team_index = lax.axis_index("team")
    rep_index = lax.axis_index("rep")
    block_rows, part_width = omega_rows.shape
    tile_width = covariance_columns.shape[1]
    all_rows = block_rows * team_count
    rows_share = all_rows // rep_count
    offset = tile_offsets[0]
    assert all_rows <= part_width and part_width % tile_width == 0
    assert rows_share % block_rows == 0 and rep_count & (rep_count - 1) == 0 and rep_count > 1

    k_ids = rep_index * part_width + jnp.arange(part_width, dtype=jnp.int32)
    c_ids = offset + jnp.arange(tile_width, dtype=jnp.int32)
    chosen = (k_ids[:, None] == c_ids[None, :]).astype(jnp.float32)
    weights = halves(chosen - step_size * covariance_columns)

    cut = part_width // 4 * 3
    assert all_rows <= cut and cut % tile_width == 0

    share_blocks = rows_share // block_rows

    def products_of(blocks, sources, spots=(), parts=()):
        start = jnp.clip(offset, 0, cut - tile_width)
        shifts = [
            jnp.where(rep_index == 0, source * block_rows - offset, 1 << 20) for source in sources
        ]
        places = jnp.stack([start, *shifts, *spots]).astype(jnp.int32)
        count, rows = (rep_count, rows_share) if spots else (len(blocks), block_rows)
        kernel = functools.partial(slots_kernel, len(blocks), len(parts))
        arrays = [*blocks, *weights, *parts]
        return call(kernel, count, (rows, tile_width), [places], arrays, 4 + len(parts) // 4)

    ring = list(range(0, team_count, 2)) + list(range(1, team_count, 2))[::-1]
    onward = [(ring[k], ring[(k + 1) % team_count]) for k in range(team_count)]
    backward = [(to, source) for source, to in onward]
    rank = team_index // 2
    place = jnp.where(team_index % 2 == 0, rank, team_count - 1 - rank)

    def device_at(spot):
        spot = spot % team_count
        up = 2 * spot
        return jnp.where(up < team_count, up, 2 * team_count - 1 - up)

    first = lax.ppermute(omega_rows, "team", onward)
    own, *weights = lax.optimization_barrier((omega_rows, *weights))
    last_step = team_count // 2
    gathered = []
    held = first
    for step in range(2, last_step):
        held = lax.ppermute(held, "team", onward)
        gathered.append((held, step))
    last_held = held
    held = own
    for step in range(1, team_count - last_step):
        held = lax.ppermute(held, "team", backward)
        gathered.append((held, -step))

    last_left = lax.ppermute(last_held[:, :cut], "team", onward)
    sources = [team_index, device_at(place - 1)]
    parts = products_of([own, first], sources)
    last_held, *parts = lax.optimization_barrier((last_held, *parts))
    last_right = lax.ppermute(last_held[:, cut:], "team", onward)
    for block, step in gathered:
        sources.append(device_at(place - step))
        parts += products_of([block], sources[-1:])
    sources.append(device_at(place - last_step))

    spots = [
        ((source // share_blocks) ^ rep_index) * share_blocks + source % share_blocks
        for source in sources
    ]
    row_spots = jnp.arange(rep_count * rows_share, dtype=jnp.int32) // block_rows
    masks = jnp.broadcast_to(
        (row_spots == spots[-1]).astype(jnp.int32).reshape(rep_count, rows_share, 1),
        (rep_count, rows_share, tile_width),
    )
    last_left, masks = lax.optimization_barrier((last_left, masks))
    shares = products_of([last_left], sources[-1:], spots, parts)
    kernel = functools.partial(last_kernel, cut)
    arrays = [masks, last_right, *weights, *shares]
    shares = call(kernel, rep_count, (rows_share, tile_width), [], arrays, 4 + rep_count)
    terms = [shares[0]]
    for flip in range(rep_count - 1, 0, -1):
        pairs = [(d, d ^ flip) for d in range(rep_count)]
        terms.append(lax.ppermute(shares[flip], "rep", pairs))
    moved = sum_of(terms)

    global_rows = rep_index * rows_share + jnp.arange(rows_share, dtype=jnp.int32)
    global_cols = offset + jnp.arange(tile_width, dtype=jnp.int32)
    diagonal = global_rows[:, None] == global_cols[None, :]
    shrunk = jnp.sign(moved) * jnp.maximum(jnp.abs(moved) - step_size * penalty, 0.0)
    return jnp.where(diagonal, moved, shrunk)


def solution(mesh):
    in_specs = (P(("groups", "team"), "rep"), P("rep", ("groups", "team")), P(("groups", "team")))
    out_specs = P("rep", ("groups", "team"))
    return jax.shard_map(
        per_device, mesh=mesh, in_specs=in_specs, out_specs=out_specs, check_vma=False
    )
```

```python
import functools

import jax
import jax.numpy as jnp
from jax import lax
from jax.experimental import pallas as pl
from jax.experimental.pallas import tpu as pltpu
from jax.sharding import PartitionSpec as P

step_size = 0.5
penalty = 0.1
largest_bf16 = 3.3895313892515355e38


def halves(array):
    high = lax.reduce_precision(jnp.clip(array, -largest_bf16, largest_bf16), 8, 7)
    return high.astype(jnp.bfloat16), (array - high).astype(jnp.bfloat16)


def products(blocks, high, low, first_k=0):
    rows, depth = blocks[0].shape
    pieces = -(-depth // 2048)
    step = depth // pieces
    assert depth % pieces == 0 and step % 128 == 0
    all_rows = rows * len(blocks)
    total = jnp.zeros((all_rows, high.shape[1]), jnp.float32)
    for k in range(0, depth, step):
        values = jnp.concatenate([block[:, k : k + step] for block in blocks], 0)
        upper = jnp.clip(values, -largest_bf16, largest_bf16).astype(jnp.bfloat16)
        lower = (values - upper.astype(jnp.float32)).astype(jnp.bfloat16)
        both = jnp.concatenate([upper, lower], 0)
        span = slice(first_k + k, first_k + k + step)
        main = jnp.dot(both, high[span], preferred_element_type=jnp.float32)
        cross = jnp.dot(upper, low[span], preferred_element_type=jnp.float32)
        total += main[:all_rows] + main[all_rows:] + cross
    return [total[b * rows : (b + 1) * rows] for b in range(len(blocks))]


def slots_kernel(blocks_count, parts_count, places, *refs):
    blocks, refs = refs[:blocks_count], refs[blocks_count:]
    high, low, *refs = refs
    parts, outs = refs[:parts_count], refs[parts_count:]
    rows, columns = blocks[0].shape[0], high.shape[1]
    totals = products(blocks, high, low)
    start = pl.multiple_of(places[0], columns)
    ahead = lax.broadcasted_iota(jnp.int32, (rows, columns), 1)
    ahead -= lax.broadcasted_iota(jnp.int32, (rows, columns), 0)
    for b, block in enumerate(blocks):
        current = block[:, pl.ds(start, columns)]
        mask = ahead == places[1 + b]
        inverse = step_size / jnp.where(mask, current, 1.0)
        totals[b] += jnp.where(mask, inverse, 0.0)
    if len(outs) == blocks_count:
        for out, value in zip(outs, totals):
            out[...] = value
        return
    per_out = outs[0].shape[0] // rows
    for o, out in enumerate(outs):
        for b in range(per_out):
            found = jnp.zeros((rows, columns), jnp.float32)
            for position, value in enumerate([part[...] for part in parts] + totals):
                mine = places[1 + blocks_count + position] == o * per_out + b
                found = found + jnp.where(mine, value, 0.0)
            out[b * rows : (b + 1) * rows] = found


def last_kernel(first_k, masks, block, high, low, *refs):
    shares, outs = refs[: len(refs) // 2], refs[len(refs) // 2 :]
    rows = block.shape[0]
    (total,) = products([block], high, low, first_k)
    for o, out in enumerate(outs):
        for b in range(out.shape[0] // rows):
            span = slice(b * rows, (b + 1) * rows)
            out[span] = shares[o][span] + jnp.where(masks[o, span] != 0, total, 0.0)


def call(kernel, count, shape, scalars, arrays, limit):
    return pl.pallas_call(
        kernel,
        out_shape=[jax.ShapeDtypeStruct(shape, jnp.float32)] * count,
        in_specs=[pl.BlockSpec(memory_space=pltpu.SMEM)] * len(scalars)
        + [pl.BlockSpec(memory_space=pltpu.VMEM)] * len(arrays),
        out_specs=[pl.BlockSpec(memory_space=pltpu.VMEM)] * count,
        compiler_params=pltpu.CompilerParams(vmem_limit_bytes=limit * 1024 * 1024),
        cost_estimate=pl.CostEstimate(
            flops=0, bytes_accessed=count * shape[0] * shape[1] * 4, transcendentals=0
        ),
    )(*scalars, *arrays)


def sum_of(terms):
    total = terms[0]
    for term in terms[1:]:
        total = total + term
    return total


def per_device(omega_rows, covariance_columns, tile_offsets):
    team_count = lax.axis_size("team")
    rep_count = lax.axis_size("rep")
    team_index = lax.axis_index("team")
    rep_index = lax.axis_index("rep")
    block_rows, part_width = omega_rows.shape
    tile_width = covariance_columns.shape[1]
    all_rows = block_rows * team_count
    rows_share = all_rows // rep_count
    offset = tile_offsets[0]
    assert all_rows <= part_width and part_width % tile_width == 0
    assert rows_share % block_rows == 0 and rep_count & (rep_count - 1) == 0 and rep_count > 1

    k_ids = rep_index * part_width + jnp.arange(part_width, dtype=jnp.int32)
    c_ids = offset + jnp.arange(tile_width, dtype=jnp.int32)
    chosen = (k_ids[:, None] == c_ids[None, :]).astype(jnp.float32)
    weights = halves(chosen - step_size * covariance_columns)

    cut = part_width // 4 * 3
    assert all_rows <= cut and cut % tile_width == 0

    share_blocks = rows_share // block_rows

    def products_of(blocks, sources, spots=(), parts=()):
        start = jnp.clip(offset, 0, cut - tile_width)
        shifts = [
            jnp.where(rep_index == 0, source * block_rows - offset, 1 << 20) for source in sources
        ]
        places = jnp.stack([start, *shifts, *spots]).astype(jnp.int32)
        count, rows = (rep_count, rows_share) if spots else (len(blocks), block_rows)
        kernel = functools.partial(slots_kernel, len(blocks), len(parts))
        arrays = [*blocks, *weights, *parts]
        return call(kernel, count, (rows, tile_width), [places], arrays, 4 + len(parts) // 4)

    ring = [0] + list(range(1, team_count, 2)) + list(range(2, team_count, 2))[::-1]
    onward = [(ring[k], ring[(k + 1) % team_count]) for k in range(team_count)]
    backward = [(to, source) for source, to in onward]
    down = (team_count - team_index // 2) % team_count
    place = jnp.where(team_index % 2 == 1, (team_index + 1) // 2, down)

    def device_at(spot):
        spot = spot % team_count
        up = 2 * spot - 1
        down = 2 * (team_count - spot) % (2 * team_count)
        return jnp.where((up > 0) & (up < team_count), up, down)

    first = lax.ppermute(omega_rows, "team", onward)
    own, *weights = lax.optimization_barrier((omega_rows, *weights))
    last_step = team_count // 2
    gathered = []
    held = first
    for step in range(2, last_step):
        held = lax.ppermute(held, "team", onward)
        gathered.append((held, step))
    last_held = held
    held = own
    for step in range(1, team_count - last_step):
        held = lax.ppermute(held, "team", backward)
        gathered.append((held, -step))

    last_left = lax.ppermute(last_held[:, :cut], "team", onward)
    sources = [team_index, device_at(place - 1)]
    parts = products_of([own, first], sources)
    last_held, *parts = lax.optimization_barrier((last_held, *parts))
    last_right = lax.ppermute(last_held[:, cut:], "team", onward)
    for block, step in gathered:
        sources.append(device_at(place - step))
        parts += products_of([block], sources[-1:])
    sources.append(device_at(place - last_step))

    spots = [
        ((source // share_blocks) ^ rep_index) * share_blocks + source % share_blocks
        for source in sources
    ]
    row_spots = jnp.arange(rep_count * rows_share, dtype=jnp.int32) // block_rows
    masks = jnp.broadcast_to(
        (row_spots == spots[-1]).astype(jnp.int32).reshape(rep_count, rows_share, 1),
        (rep_count, rows_share, tile_width),
    )
    last_left, masks = lax.optimization_barrier((last_left, masks))
    shares = products_of([last_left], sources[-1:], spots, parts)
    kernel = functools.partial(last_kernel, cut)
    arrays = [masks, last_right, *weights, *shares]
    shares = call(kernel, rep_count, (rows_share, tile_width), [], arrays, 4 + rep_count)
    terms = [shares[0]]
    for flip in range(rep_count - 1, 0, -1):
        pairs = [(d, d ^ flip) for d in range(rep_count)]
        terms.append(lax.ppermute(shares[flip], "rep", pairs))
    moved = sum_of(terms)

    global_rows = rep_index * rows_share + jnp.arange(rows_share, dtype=jnp.int32)
    global_cols = offset + jnp.arange(tile_width, dtype=jnp.int32)
    diagonal = global_rows[:, None] == global_cols[None, :]
    shrunk = jnp.sign(moved) * jnp.maximum(jnp.abs(moved) - step_size * penalty, 0.0)
    return jnp.where(diagonal, moved, shrunk)


def solution(mesh):
    in_specs = (P(("groups", "team"), "rep"), P("rep", ("groups", "team")), P(("groups", "team")))
    out_specs = P("rep", ("groups", "team"))
    return jax.shard_map(
        per_device, mesh=mesh, in_specs=in_specs, out_specs=out_specs, check_vma=False
    )
```

```python
import functools
import math

import jax
import jax.numpy as jnp
from jax import lax
from jax.experimental import pallas as pl
from jax.experimental.pallas import tpu as pltpu
from jax.sharding import PartitionSpec as P

step_size = 0.5
penalty = 0.1
largest_bf16 = 3.3895313892515355e38


def weights_kernel(shift, covariance, high, low, held, arrived):
    depth, columns = covariance.shape
    step = held.shape[1]
    pieces = depth // step

    def copy(piece):
        return pltpu.make_async_copy(
            covariance.at[pl.ds(piece * step, step)], held.at[piece % 4], arrived.at[piece % 4]
        )

    for piece in range(min(3, pieces)):
        copy(piece).start()
    ahead = lax.broadcasted_iota(jnp.int32, (step, columns), 0)
    ahead -= lax.broadcasted_iota(jnp.int32, (step, columns), 1)
    for piece in range(pieces):
        if piece + 3 < pieces:
            copy(piece + 3).start()
        copy(piece).wait()
        scaled = -step_size * held[piece % 4]
        values = jnp.where(ahead == shift[0] - piece * step, scaled + 1.0, scaled)
        upper = values.astype(jnp.bfloat16)
        rows = slice(piece * step, (piece + 1) * step)
        high[rows] = upper
        low[rows] = (values - upper.astype(jnp.float32)).astype(jnp.bfloat16)


def weights_of(covariance, shift):
    depth, columns = covariance.shape
    step = math.gcd(depth, 512)
    return pl.pallas_call(
        weights_kernel,
        out_shape=[pltpu.VMEM((depth, columns), jnp.bfloat16)] * 2,
        in_specs=[
            pl.BlockSpec(memory_space=pltpu.SMEM),
            pl.BlockSpec(memory_space=pltpu.HBM),
        ],
        out_specs=[pl.BlockSpec(memory_space=pltpu.VMEM)] * 2,
        scratch_shapes=[
            pltpu.VMEM((4, step, columns), jnp.float32),
            pltpu.SemaphoreType.DMA((4,)),
        ],
        compiler_params=pltpu.CompilerParams(vmem_limit_bytes=8 * 1024 * 1024),
        cost_estimate=pl.CostEstimate(
            flops=0, bytes_accessed=covariance.size * 4, transcendentals=0
        ),
    )(shift, pltpu.with_memory_space_constraint(covariance, pltpu.HBM))


def products(blocks, high, low, first_k=0):
    rows, depth = blocks[0].shape
    pieces = -(-depth // 2048)
    step = depth // pieces
    assert depth % pieces == 0 and step % 128 == 0
    all_rows = rows * len(blocks)
    total = jnp.zeros((all_rows, high.shape[1]), jnp.float32)
    for k in range(0, depth, step):
        values = jnp.concatenate([block[:, k : k + step] for block in blocks], 0)
        upper = jnp.clip(values, -largest_bf16, largest_bf16).astype(jnp.bfloat16)
        lower = (values - upper.astype(jnp.float32)).astype(jnp.bfloat16)
        both = jnp.concatenate([upper, lower], 0)
        span = slice(first_k + k, first_k + k + step)
        main = jnp.dot(both, high[span], preferred_element_type=jnp.float32)
        cross = jnp.dot(upper, low[span], preferred_element_type=jnp.float32)
        total += main[:all_rows] + main[all_rows:] + cross
    return [total[b * rows : (b + 1) * rows] for b in range(len(blocks))]


def slots_kernel(blocks_count, parts_count, places, *refs):
    blocks, refs = refs[:blocks_count], refs[blocks_count:]
    high, low, *refs = refs
    parts, outs = refs[:parts_count], refs[parts_count:]
    rows, columns = blocks[0].shape[0], high.shape[1]
    totals = products(blocks, high, low)
    start = pl.multiple_of(places[0], columns)
    ahead = lax.broadcasted_iota(jnp.int32, (rows, columns), 1)
    ahead -= lax.broadcasted_iota(jnp.int32, (rows, columns), 0)
    for b, block in enumerate(blocks):
        current = block[:, pl.ds(start, columns)]
        mask = ahead == places[1 + b]
        inverse = step_size / jnp.where(mask, current, 1.0)
        totals[b] += jnp.where(mask, inverse, 0.0)
    if len(outs) == blocks_count:
        for out, value in zip(outs, totals):
            out[...] = value
        return
    per_out = outs[0].shape[0] // rows
    for o, out in enumerate(outs):
        for b in range(per_out):
            found = jnp.zeros((rows, columns), jnp.float32)
            for position, value in enumerate([part[...] for part in parts] + totals):
                mine = places[1 + blocks_count + position] == o * per_out + b
                found = found + jnp.where(mine, value, 0.0)
            out[b * rows : (b + 1) * rows] = found


def last_kernel(first_k, masks, block, high, low, *refs):
    shares, outs = refs[: len(refs) // 2], refs[len(refs) // 2 :]
    rows = block.shape[0]
    (total,) = products([block], high, low, first_k)
    for o, out in enumerate(outs):
        for b in range(out.shape[0] // rows):
            span = slice(b * rows, (b + 1) * rows)
            out[span] = shares[o][span] + jnp.where(masks[o, span] != 0, total, 0.0)


def call(kernel, count, shape, scalars, arrays, limit):
    return pl.pallas_call(
        kernel,
        out_shape=[jax.ShapeDtypeStruct(shape, jnp.float32)] * count,
        in_specs=[pl.BlockSpec(memory_space=pltpu.SMEM)] * len(scalars)
        + [pl.BlockSpec(memory_space=pltpu.VMEM)] * len(arrays),
        out_specs=[pl.BlockSpec(memory_space=pltpu.VMEM)] * count,
        compiler_params=pltpu.CompilerParams(vmem_limit_bytes=limit * 1024 * 1024),
        cost_estimate=pl.CostEstimate(
            flops=0, bytes_accessed=count * shape[0] * shape[1] * 4, transcendentals=0
        ),
    )(*scalars, *arrays)


def sum_of(terms):
    total = terms[0]
    for term in terms[1:]:
        total = total + term
    return total


def per_device(omega_rows, covariance_columns, tile_offsets):
    team_count = lax.axis_size("team")
    rep_count = lax.axis_size("rep")
    team_index = lax.axis_index("team")
    rep_index = lax.axis_index("rep")
    block_rows, part_width = omega_rows.shape
    tile_width = covariance_columns.shape[1]
    all_rows = block_rows * team_count
    rows_share = all_rows // rep_count
    offset = tile_offsets[0]
    assert all_rows <= part_width and part_width % tile_width == 0
    assert rows_share % block_rows == 0 and rep_count & (rep_count - 1) == 0 and rep_count > 1

    shift = jnp.reshape(offset - rep_index * part_width, (1,)).astype(jnp.int32)
    weights = weights_of(covariance_columns, shift)

    cut = part_width // 4 * 3
    assert all_rows <= cut and cut % tile_width == 0

    share_blocks = rows_share // block_rows

    def products_of(blocks, sources, spots=(), parts=()):
        start = jnp.clip(offset, 0, cut - tile_width)
        shifts = [
            jnp.where(rep_index == 0, source * block_rows - offset, 1 << 20) for source in sources
        ]
        places = jnp.stack([start, *shifts, *spots]).astype(jnp.int32)
        count, rows = (rep_count, rows_share) if spots else (len(blocks), block_rows)
        kernel = functools.partial(slots_kernel, len(blocks), len(parts))
        arrays = [*blocks, *weights, *parts]
        return call(kernel, count, (rows, tile_width), [places], arrays, 4 + len(parts) // 4)

    ring = list(range(0, team_count, 2)) + list(range(1, team_count, 2))[::-1]
    onward = [(ring[k], ring[(k + 1) % team_count]) for k in range(team_count)]
    backward = [(to, source) for source, to in onward]
    rank = team_index // 2
    place = jnp.where(team_index % 2 == 0, rank, team_count - 1 - rank)

    def device_at(spot):
        spot = spot % team_count
        up = 2 * spot
        return jnp.where(up < team_count, up, 2 * team_count - 1 - up)

    first = lax.ppermute(omega_rows, "team", onward)
    own, *weights = lax.optimization_barrier((omega_rows, *weights))
    last_step = team_count // 2
    gathered = []
    held = first
    for step in range(2, last_step):
        held = lax.ppermute(held, "team", onward)
        gathered.append((held, step))
    last_held = held
    held = own
    for step in range(1, team_count - last_step):
        held = lax.ppermute(held, "team", backward)
        gathered.append((held, -step))

    last_left = lax.ppermute(last_held[:, :cut], "team", onward)
    sources = [team_index, device_at(place - 1)]
    parts = products_of([own, first], sources)
    last_held, *parts = lax.optimization_barrier((last_held, *parts))
    last_right = lax.ppermute(last_held[:, cut:], "team", onward)
    for block, step in gathered:
        sources.append(device_at(place - step))
        parts += products_of([block], sources[-1:])
    sources.append(device_at(place - last_step))

    spots = [
        ((source // share_blocks) ^ rep_index) * share_blocks + source % share_blocks
        for source in sources
    ]
    row_spots = jnp.arange(rep_count * rows_share, dtype=jnp.int32) // block_rows
    masks = jnp.broadcast_to(
        (row_spots == spots[-1]).astype(jnp.int32).reshape(rep_count, rows_share, 1),
        (rep_count, rows_share, tile_width),
    )
    last_left, masks = lax.optimization_barrier((last_left, masks))
    shares = products_of([last_left], sources[-1:], spots, parts)
    kernel = functools.partial(last_kernel, cut)
    arrays = [masks, last_right, *weights, *shares]
    shares = call(kernel, rep_count, (rows_share, tile_width), [], arrays, 4 + rep_count)
    terms = [shares[0]]
    for flip in range(rep_count - 1, 0, -1):
        pairs = [(d, d ^ flip) for d in range(rep_count)]
        terms.append(lax.ppermute(shares[flip], "rep", pairs))
    moved = sum_of(terms)

    global_rows = rep_index * rows_share + jnp.arange(rows_share, dtype=jnp.int32)
    global_cols = offset + jnp.arange(tile_width, dtype=jnp.int32)
    diagonal = global_rows[:, None] == global_cols[None, :]
    shrunk = jnp.sign(moved) * jnp.maximum(jnp.abs(moved) - step_size * penalty, 0.0)
    return jnp.where(diagonal, moved, shrunk)


def solution(mesh):
    in_specs = (P(("groups", "team"), "rep"), P("rep", ("groups", "team")), P(("groups", "team")))
    out_specs = P("rep", ("groups", "team"))
    return jax.shard_map(
        per_device, mesh=mesh, in_specs=in_specs, out_specs=out_specs, check_vma=False
    )
```

```python
import functools
import math

import jax
import jax.numpy as jnp
from jax import lax
from jax.experimental import pallas as pl
from jax.experimental.pallas import tpu as pltpu
from jax.sharding import PartitionSpec as P

step_size = 0.5
penalty = 0.1
largest_bf16 = 3.3895313892515355e38


def weights_kernel(shift, covariance, high, low, ticket, held, arrived):
    depth, columns = covariance.shape
    step = held.shape[1]
    pieces = depth // step

    def copy(piece):
        return pltpu.make_async_copy(
            covariance.at[pl.ds(piece * step, step)], held.at[piece % 4], arrived.at[piece % 4]
        )

    for piece in range(min(3, pieces)):
        copy(piece).start()
    ahead = lax.broadcasted_iota(jnp.int32, (step, columns), 0)
    ahead -= lax.broadcasted_iota(jnp.int32, (step, columns), 1)
    for piece in range(pieces):
        if piece + 3 < pieces:
            copy(piece + 3).start()
        copy(piece).wait()
        scaled = -step_size * held[piece % 4]
        values = jnp.where(ahead == shift[0] - piece * step, scaled + 1.0, scaled)
        upper = values.astype(jnp.bfloat16)
        rows = slice(piece * step, (piece + 1) * step)
        high[rows] = upper
        low[rows] = (values - upper.astype(jnp.float32)).astype(jnp.bfloat16)
    ticket[...] = jnp.zeros(ticket.shape, jnp.float32)


def weights_of(covariance, shift):
    depth, columns = covariance.shape
    step = math.gcd(depth, 512)
    return pl.pallas_call(
        weights_kernel,
        out_shape=[pltpu.VMEM((depth, columns), jnp.bfloat16)] * 2
        + [jax.ShapeDtypeStruct((8, 128), jnp.float32)],
        in_specs=[
            pl.BlockSpec(memory_space=pltpu.SMEM),
            pl.BlockSpec(memory_space=pltpu.HBM),
        ],
        out_specs=[pl.BlockSpec(memory_space=pltpu.VMEM)] * 3,
        scratch_shapes=[
            pltpu.VMEM((4, step, columns), jnp.float32),
            pltpu.SemaphoreType.DMA((4,)),
        ],
        compiler_params=pltpu.CompilerParams(vmem_limit_bytes=8 * 1024 * 1024),
        cost_estimate=pl.CostEstimate(
            flops=0, bytes_accessed=covariance.size * 4, transcendentals=0
        ),
    )(shift, pltpu.with_memory_space_constraint(covariance, pltpu.HBM))


def products(blocks, high, low, first_k=0):
    rows, depth = blocks[0].shape
    pieces = -(-depth // 2048)
    step = depth // pieces
    assert depth % pieces == 0 and step % 128 == 0
    all_rows = rows * len(blocks)
    total = jnp.zeros((all_rows, high.shape[1]), jnp.float32)
    for k in range(0, depth, step):
        values = jnp.concatenate([block[:, k : k + step] for block in blocks], 0)
        upper = jnp.clip(values, -largest_bf16, largest_bf16).astype(jnp.bfloat16)
        lower = (values - upper.astype(jnp.float32)).astype(jnp.bfloat16)
        both = jnp.concatenate([upper, lower], 0)
        span = slice(first_k + k, first_k + k + step)
        main = jnp.dot(both, high[span], preferred_element_type=jnp.float32)
        cross = jnp.dot(upper, low[span], preferred_element_type=jnp.float32)
        total += main[:all_rows] + main[all_rows:] + cross
    return [total[b * rows : (b + 1) * rows] for b in range(len(blocks))]


def slots_kernel(blocks_count, parts_count, places, *refs):
    blocks, refs = refs[:blocks_count], refs[blocks_count:]
    high, low, *refs = refs
    parts, outs = refs[:parts_count], refs[parts_count:]
    rows, columns = blocks[0].shape[0], high.shape[1]
    totals = products(blocks, high, low)
    start = pl.multiple_of(places[0], columns)
    ahead = lax.broadcasted_iota(jnp.int32, (rows, columns), 1)
    ahead -= lax.broadcasted_iota(jnp.int32, (rows, columns), 0)
    for b, block in enumerate(blocks):
        current = block[:, pl.ds(start, columns)]
        mask = ahead == places[1 + b]
        inverse = step_size / jnp.where(mask, current, 1.0)
        totals[b] += jnp.where(mask, inverse, 0.0)
    if len(outs) == blocks_count:
        for out, value in zip(outs, totals):
            out[...] = value
        return
    per_out = outs[0].shape[0] // rows
    for o, out in enumerate(outs):
        for b in range(per_out):
            found = jnp.zeros((rows, columns), jnp.float32)
            for position, value in enumerate([part[...] for part in parts] + totals):
                mine = places[1 + blocks_count + position] == o * per_out + b
                found = found + jnp.where(mine, value, 0.0)
            out[b * rows : (b + 1) * rows] = found


def last_kernel(first_k, masks, block, high, low, *refs):
    shares, outs = refs[: len(refs) // 2], refs[len(refs) // 2 :]
    rows = block.shape[0]
    (total,) = products([block], high, low, first_k)
    for o, out in enumerate(outs):
        for b in range(out.shape[0] // rows):
            span = slice(b * rows, (b + 1) * rows)
            out[span] = shares[o][span] + jnp.where(masks[o, span] != 0, total, 0.0)


def call(kernel, count, shape, scalars, arrays, limit):
    return pl.pallas_call(
        kernel,
        out_shape=[jax.ShapeDtypeStruct(shape, jnp.float32)] * count,
        in_specs=[pl.BlockSpec(memory_space=pltpu.SMEM)] * len(scalars)
        + [pl.BlockSpec(memory_space=pltpu.VMEM)] * len(arrays),
        out_specs=[pl.BlockSpec(memory_space=pltpu.VMEM)] * count,
        compiler_params=pltpu.CompilerParams(vmem_limit_bytes=limit * 1024 * 1024),
        cost_estimate=pl.CostEstimate(
            flops=0, bytes_accessed=count * shape[0] * shape[1] * 4, transcendentals=0
        ),
    )(*scalars, *arrays)


def sum_of(terms):
    total = terms[0]
    for term in terms[1:]:
        total = total + term
    return total


def per_device(omega_rows, covariance_columns, tile_offsets):
    team_count = lax.axis_size("team")
    rep_count = lax.axis_size("rep")
    team_index = lax.axis_index("team")
    rep_index = lax.axis_index("rep")
    block_rows, part_width = omega_rows.shape
    tile_width = covariance_columns.shape[1]
    all_rows = block_rows * team_count
    rows_share = all_rows // rep_count
    offset = tile_offsets[0]
    assert all_rows <= part_width and part_width % tile_width == 0
    assert rows_share % block_rows == 0 and rep_count & (rep_count - 1) == 0 and rep_count > 1

    shift = jnp.reshape(offset - rep_index * part_width, (1,)).astype(jnp.int32)
    *weights, ticket = weights_of(covariance_columns, shift)

    cut = part_width // 4 * 3
    assert all_rows <= cut and cut % tile_width == 0

    share_blocks = rows_share // block_rows

    def products_of(blocks, sources, spots=(), parts=()):
        start = jnp.clip(offset, 0, cut - tile_width)
        shifts = [
            jnp.where(rep_index == 0, source * block_rows - offset, 1 << 20) for source in sources
        ]
        places = jnp.stack([start, *shifts, *spots]).astype(jnp.int32)
        count, rows = (rep_count, rows_share) if spots else (len(blocks), block_rows)
        kernel = functools.partial(slots_kernel, len(blocks), len(parts))
        arrays = [*blocks, *weights, *parts]
        return call(kernel, count, (rows, tile_width), [places], arrays, 4 + len(parts) // 4)

    ring = list(range(0, team_count, 2)) + list(range(1, team_count, 2))[::-1]
    onward = [(ring[k], ring[(k + 1) % team_count]) for k in range(team_count)]
    backward = [(to, source) for source, to in onward]
    rank = team_index // 2
    place = jnp.where(team_index % 2 == 0, rank, team_count - 1 - rank)

    def device_at(spot):
        spot = spot % team_count
        up = 2 * spot
        return jnp.where(up < team_count, up, 2 * team_count - 1 - up)

    first = lax.ppermute(omega_rows, "team", onward)
    own, _ = lax.optimization_barrier((omega_rows, ticket))
    last_step = team_count // 2
    gathered = []
    held = first
    for step in range(2, last_step):
        held = lax.ppermute(held, "team", onward)
        gathered.append((held, step))
    last_held = held
    held = own
    for step in range(1, team_count - last_step):
        held = lax.ppermute(held, "team", backward)
        gathered.append((held, -step))

    last_left = lax.ppermute(last_held[:, :cut], "team", onward)
    sources = [team_index, device_at(place - 1)]
    parts = products_of([own, first], sources)
    last_held, *parts = lax.optimization_barrier((last_held, *parts))
    last_right = lax.ppermute(last_held[:, cut:], "team", onward)
    for block, step in gathered:
        sources.append(device_at(place - step))
        parts += products_of([block], sources[-1:])
    sources.append(device_at(place - last_step))

    spots = [
        ((source // share_blocks) ^ rep_index) * share_blocks + source % share_blocks
        for source in sources
    ]
    row_spots = jnp.arange(rep_count * rows_share, dtype=jnp.int32) // block_rows
    masks = jnp.broadcast_to(
        (row_spots == spots[-1]).astype(jnp.int32).reshape(rep_count, rows_share, 1),
        (rep_count, rows_share, tile_width),
    )
    last_left, masks = lax.optimization_barrier((last_left, masks))
    shares = products_of([last_left], sources[-1:], spots, parts)
    kernel = functools.partial(last_kernel, cut)
    arrays = [masks, last_right, *weights, *shares]
    shares = call(kernel, rep_count, (rows_share, tile_width), [], arrays, 4 + rep_count)
    terms = [shares[0]]
    for flip in range(rep_count - 1, 0, -1):
        pairs = [(d, d ^ flip) for d in range(rep_count)]
        terms.append(lax.ppermute(shares[flip], "rep", pairs))
    moved = sum_of(terms)

    global_rows = rep_index * rows_share + jnp.arange(rows_share, dtype=jnp.int32)
    global_cols = offset + jnp.arange(tile_width, dtype=jnp.int32)
    diagonal = global_rows[:, None] == global_cols[None, :]
    shrunk = jnp.sign(moved) * jnp.maximum(jnp.abs(moved) - step_size * penalty, 0.0)
    return jnp.where(diagonal, moved, shrunk)


def solution(mesh):
    in_specs = (P(("groups", "team"), "rep"), P("rep", ("groups", "team")), P(("groups", "team")))
    out_specs = P("rep", ("groups", "team"))
    return jax.shard_map(
        per_device, mesh=mesh, in_specs=in_specs, out_specs=out_specs, check_vma=False
    )
```

```python
import functools

import jax
import jax.numpy as jnp
from jax import lax
from jax.experimental import pallas as pl
from jax.experimental.pallas import tpu as pltpu
from jax.sharding import PartitionSpec as P

step_size = 0.5
penalty = 0.1
largest_bf16 = 3.3895313892515355e38


def halves(array):
    high = lax.reduce_precision(jnp.clip(array, -largest_bf16, largest_bf16), 8, 7)
    return high.astype(jnp.bfloat16), (array - high).astype(jnp.bfloat16)


def products(blocks, high, low, first_k=0):
    rows, depth = blocks[0].shape
    pieces = -(-depth // 2048)
    step = depth // pieces
    assert depth % pieces == 0 and step % 128 == 0
    all_rows = rows * len(blocks)
    total = jnp.zeros((all_rows, high.shape[1]), jnp.float32)
    for k in range(0, depth, step):
        values = jnp.concatenate([block[:, k : k + step] for block in blocks], 0)
        upper = jnp.clip(values, -largest_bf16, largest_bf16).astype(jnp.bfloat16)
        lower = (values - upper.astype(jnp.float32)).astype(jnp.bfloat16)
        both = jnp.concatenate([upper, lower], 0)
        span = slice(first_k + k, first_k + k + step)
        main = jnp.dot(both, high[span], preferred_element_type=jnp.float32)
        cross = jnp.dot(upper, low[span], preferred_element_type=jnp.float32)
        total += main[:all_rows] + main[all_rows:] + cross
    return [total[b * rows : (b + 1) * rows] for b in range(len(blocks))]


def slots_kernel(blocks_count, parts_count, places, *refs):
    blocks, refs = refs[:blocks_count], refs[blocks_count:]
    high, low, *refs = refs
    parts, outs = refs[:parts_count], refs[parts_count:]
    rows, columns = blocks[0].shape[0], high.shape[1]
    totals = products(blocks, high, low)
    start = pl.multiple_of(places[0], columns)
    ahead = lax.broadcasted_iota(jnp.int32, (rows, columns), 1)
    ahead -= lax.broadcasted_iota(jnp.int32, (rows, columns), 0)
    for b, block in enumerate(blocks):
        current = block[:, pl.ds(start, columns)]
        mask = ahead == places[1 + b]
        inverse = step_size / jnp.where(mask, current, 1.0)
        totals[b] += jnp.where(mask, inverse, 0.0)
    if len(outs) == blocks_count:
        for out, value in zip(outs, totals):
            out[...] = value
        return
    per_out = outs[0].shape[0] // rows
    for o, out in enumerate(outs):
        for b in range(per_out):
            found = jnp.zeros((rows, columns), jnp.float32)
            for position, value in enumerate([part[...] for part in parts] + totals):
                mine = places[1 + blocks_count + position] == o * per_out + b
                found = found + jnp.where(mine, value, 0.0)
            out[b * rows : (b + 1) * rows] = found


def last_kernel(first_k, masks, block, high, low, *refs):
    shares, outs = refs[: len(refs) // 2], refs[len(refs) // 2 :]
    rows = block.shape[0]
    (total,) = products([block], high, low, first_k)
    for o, out in enumerate(outs):
        for b in range(out.shape[0] // rows):
            span = slice(b * rows, (b + 1) * rows)
            out[span] = shares[o][span] + jnp.where(masks[o, span] != 0, total, 0.0)


def call(kernel, count, shape, scalars, arrays, limit):
    return pl.pallas_call(
        kernel,
        out_shape=[jax.ShapeDtypeStruct(shape, jnp.float32)] * count,
        in_specs=[pl.BlockSpec(memory_space=pltpu.SMEM)] * len(scalars)
        + [pl.BlockSpec(memory_space=pltpu.VMEM)] * len(arrays),
        out_specs=[pl.BlockSpec(memory_space=pltpu.VMEM)] * count,
        compiler_params=pltpu.CompilerParams(vmem_limit_bytes=limit * 1024 * 1024),
        cost_estimate=pl.CostEstimate(
            flops=0, bytes_accessed=count * shape[0] * shape[1] * 4, transcendentals=0
        ),
    )(*scalars, *arrays)


def sum_of(terms):
    total = terms[0]
    for term in terms[1:]:
        total = total + term
    return total


def per_device(omega_rows, covariance_columns, tile_offsets):
    team_count = lax.axis_size("team")
    rep_count = lax.axis_size("rep")
    team_index = lax.axis_index("team")
    rep_index = lax.axis_index("rep")
    block_rows, part_width = omega_rows.shape
    tile_width = covariance_columns.shape[1]
    all_rows = block_rows * team_count
    rows_share = all_rows // rep_count
    offset = tile_offsets[0]
    assert all_rows <= part_width and part_width % tile_width == 0
    assert rows_share % block_rows == 0 and rep_count & (rep_count - 1) == 0 and rep_count > 1

    k_ids = rep_index * part_width + jnp.arange(part_width, dtype=jnp.int32)
    c_ids = offset + jnp.arange(tile_width, dtype=jnp.int32)
    chosen = (k_ids[:, None] == c_ids[None, :]).astype(jnp.float32)
    weights = halves(chosen - step_size * covariance_columns)

    cut = part_width // 4 * 3
    assert all_rows <= cut and cut % tile_width == 0

    share_blocks = rows_share // block_rows

    def products_of(blocks, sources, spots=(), parts=()):
        start = jnp.clip(offset, 0, cut - tile_width)
        shifts = [
            jnp.where(rep_index == 0, source * block_rows - offset, 1 << 20) for source in sources
        ]
        places = jnp.stack([start, *shifts, *spots]).astype(jnp.int32)
        count, rows = (rep_count, rows_share) if spots else (len(blocks), block_rows)
        kernel = functools.partial(slots_kernel, len(blocks), len(parts))
        arrays = [*blocks, *weights, *parts]
        return call(kernel, count, (rows, tile_width), [places], arrays, 4 + len(parts) // 4)

    ring = list(range(0, team_count, 2)) + list(range(1, team_count, 2))[::-1]
    onward = [(ring[k], ring[(k + 1) % team_count]) for k in range(team_count)]
    backward = [(to, source) for source, to in onward]
    rank = team_index // 2
    place = jnp.where(team_index % 2 == 0, rank, team_count - 1 - rank)

    def device_at(spot):
        spot = spot % team_count
        up = 2 * spot
        return jnp.where(up < team_count, up, 2 * team_count - 1 - up)

    first = lax.ppermute(omega_rows, "team", onward)
    own = omega_rows
    last_step = team_count // 2
    gathered = []
    held = first
    for step in range(2, last_step):
        held = lax.ppermute(held, "team", onward)
        gathered.append((held, step))
    last_held = held
    held = own
    for step in range(1, team_count - last_step):
        held = lax.ppermute(held, "team", backward)
        gathered.append((held, -step))

    last_left = lax.ppermute(last_held[:, :cut], "team", onward)
    sources = [team_index, device_at(place - 1)]
    parts = products_of([own, first], sources)
    last_held, *parts = lax.optimization_barrier((last_held, *parts))
    last_right = lax.ppermute(last_held[:, cut:], "team", onward)
    for block, step in gathered:
        sources.append(device_at(place - step))
        parts += products_of([block], sources[-1:])
    sources.append(device_at(place - last_step))

    spots = [
        ((source // share_blocks) ^ rep_index) * share_blocks + source % share_blocks
        for source in sources
    ]
    row_spots = jnp.arange(rep_count * rows_share, dtype=jnp.int32) // block_rows
    masks = jnp.broadcast_to(
        (row_spots == spots[-1]).astype(jnp.int32).reshape(rep_count, rows_share, 1),
        (rep_count, rows_share, tile_width),
    )
    last_left, masks = lax.optimization_barrier((last_left, masks))
    shares = products_of([last_left], sources[-1:], spots, parts)
    kernel = functools.partial(last_kernel, cut)
    arrays = [masks, last_right, *weights, *shares]
    shares = call(kernel, rep_count, (rows_share, tile_width), [], arrays, 4 + rep_count)
    terms = [shares[0]]
    for flip in range(rep_count - 1, 0, -1):
        pairs = [(d, d ^ flip) for d in range(rep_count)]
        terms.append(lax.ppermute(shares[flip], "rep", pairs))
    moved = sum_of(terms)

    global_rows = rep_index * rows_share + jnp.arange(rows_share, dtype=jnp.int32)
    global_cols = offset + jnp.arange(tile_width, dtype=jnp.int32)
    diagonal = global_rows[:, None] == global_cols[None, :]
    shrunk = jnp.sign(moved) * jnp.maximum(jnp.abs(moved) - step_size * penalty, 0.0)
    return jnp.where(diagonal, moved, shrunk)


def solution(mesh):
    in_specs = (P(("groups", "team"), "rep"), P("rep", ("groups", "team")), P(("groups", "team")))
    out_specs = P("rep", ("groups", "team"))
    return jax.shard_map(
        per_device, mesh=mesh, in_specs=in_specs, out_specs=out_specs, check_vma=False
    )
```

```python
import functools

import jax
import jax.numpy as jnp
from jax import lax
from jax.experimental import pallas as pl
from jax.experimental.pallas import tpu as pltpu
from jax.sharding import PartitionSpec as P

step_size = 0.5
penalty = 0.1
largest_bf16 = 3.3895313892515355e38


def halves(array):
    high = lax.reduce_precision(jnp.clip(array, -largest_bf16, largest_bf16), 8, 7)
    return high.astype(jnp.bfloat16), (array - high).astype(jnp.bfloat16)


def products(blocks, high, low, first_k=0):
    rows, depth = blocks[0].shape
    pieces = -(-depth // 2048)
    step = depth // pieces
    assert depth % pieces == 0 and step % 128 == 0
    all_rows = rows * len(blocks)
    total = jnp.zeros((all_rows, high.shape[1]), jnp.float32)
    for k in range(0, depth, step):
        values = jnp.concatenate([block[:, k : k + step] for block in blocks], 0)
        upper = jnp.clip(values, -largest_bf16, largest_bf16).astype(jnp.bfloat16)
        lower = (values - upper.astype(jnp.float32)).astype(jnp.bfloat16)
        both = jnp.concatenate([upper, lower], 0)
        span = slice(first_k + k, first_k + k + step)
        main = jnp.dot(both, high[span], preferred_element_type=jnp.float32)
        cross = jnp.dot(upper, low[span], preferred_element_type=jnp.float32)
        total += main[:all_rows] + main[all_rows:] + cross
    return [total[b * rows : (b + 1) * rows] for b in range(len(blocks))]


def slots_kernel(blocks_count, parts_count, places, *refs):
    blocks, refs = refs[:blocks_count], refs[blocks_count:]
    high, low, *refs = refs
    parts, outs = refs[:parts_count], refs[parts_count:]
    rows, columns = blocks[0].shape[0], high.shape[1]
    totals = products(blocks, high, low)
    start = pl.multiple_of(places[0], columns)
    ahead = lax.broadcasted_iota(jnp.int32, (rows, columns), 1)
    ahead -= lax.broadcasted_iota(jnp.int32, (rows, columns), 0)
    for b, block in enumerate(blocks):
        current = block[:, pl.ds(start, columns)]
        mask = ahead == places[1 + b]
        inverse = step_size / jnp.where(mask, current, 1.0)
        totals[b] += jnp.where(mask, inverse, 0.0)
    if len(outs) == blocks_count:
        for out, value in zip(outs, totals):
            out[...] = value
        return
    per_out = outs[0].shape[0] // rows
    for o, out in enumerate(outs):
        for b in range(per_out):
            found = jnp.zeros((rows, columns), jnp.float32)
            for position, value in enumerate([part[...] for part in parts] + totals):
                mine = places[1 + blocks_count + position] == o * per_out + b
                found = found + jnp.where(mine, value, 0.0)
            out[b * rows : (b + 1) * rows] = found


def last_kernel(first_k, masks, block, high, low, *refs):
    shares, outs = refs[: len(refs) // 2], refs[len(refs) // 2 :]
    rows = block.shape[0]
    (total,) = products([block], high, low, first_k)
    for o, out in enumerate(outs):
        for b in range(out.shape[0] // rows):
            span = slice(b * rows, (b + 1) * rows)
            out[span] = shares[o][span] + jnp.where(masks[o, span] != 0, total, 0.0)


def final_kernel(diagonal, *refs):
    *terms, out = refs
    moved = sum_of([term[...] for term in terms])
    limit = step_size * penalty
    shrunk = jnp.maximum(moved - limit, 0.0) + jnp.minimum(moved + limit, 0.0)
    out[...] = jnp.where(diagonal[...] != 0, moved, shrunk)


def call(kernel, count, shape, scalars, arrays, limit):
    return pl.pallas_call(
        kernel,
        out_shape=[jax.ShapeDtypeStruct(shape, jnp.float32)] * count,
        in_specs=[pl.BlockSpec(memory_space=pltpu.SMEM)] * len(scalars)
        + [pl.BlockSpec(memory_space=pltpu.VMEM)] * len(arrays),
        out_specs=[pl.BlockSpec(memory_space=pltpu.VMEM)] * count,
        compiler_params=pltpu.CompilerParams(vmem_limit_bytes=limit * 1024 * 1024),
        cost_estimate=pl.CostEstimate(
            flops=0, bytes_accessed=count * shape[0] * shape[1] * 4, transcendentals=0
        ),
    )(*scalars, *arrays)


def sum_of(terms):
    total = terms[0]
    for term in terms[1:]:
        total = total + term
    return total


def per_device(omega_rows, covariance_columns, tile_offsets):
    team_count = lax.axis_size("team")
    rep_count = lax.axis_size("rep")
    team_index = lax.axis_index("team")
    rep_index = lax.axis_index("rep")
    block_rows, part_width = omega_rows.shape
    tile_width = covariance_columns.shape[1]
    all_rows = block_rows * team_count
    rows_share = all_rows // rep_count
    offset = tile_offsets[0]
    assert all_rows <= part_width and part_width % tile_width == 0
    assert rows_share % block_rows == 0 and rep_count & (rep_count - 1) == 0 and rep_count > 1

    k_ids = rep_index * part_width + jnp.arange(part_width, dtype=jnp.int32)
    c_ids = offset + jnp.arange(tile_width, dtype=jnp.int32)
    chosen = (k_ids[:, None] == c_ids[None, :]).astype(jnp.float32)
    weights = halves(chosen - step_size * covariance_columns)

    cut = part_width // 4 * 3
    assert all_rows <= cut and cut % tile_width == 0

    share_blocks = rows_share // block_rows

    def products_of(blocks, sources, spots=(), parts=()):
        start = jnp.clip(offset, 0, cut - tile_width)
        shifts = [
            jnp.where(rep_index == 0, source * block_rows - offset, 1 << 20) for source in sources
        ]
        places = jnp.stack([start, *shifts, *spots]).astype(jnp.int32)
        count, rows = (rep_count, rows_share) if spots else (len(blocks), block_rows)
        kernel = functools.partial(slots_kernel, len(blocks), len(parts))
        arrays = [*blocks, *weights, *parts]
        return call(kernel, count, (rows, tile_width), [places], arrays, 4 + len(parts) // 4)

    ring = list(range(0, team_count, 2)) + list(range(1, team_count, 2))[::-1]
    onward = [(ring[k], ring[(k + 1) % team_count]) for k in range(team_count)]
    backward = [(to, source) for source, to in onward]
    rank = team_index // 2
    place = jnp.where(team_index % 2 == 0, rank, team_count - 1 - rank)

    def device_at(spot):
        spot = spot % team_count
        up = 2 * spot
        return jnp.where(up < team_count, up, 2 * team_count - 1 - up)

    first = lax.ppermute(omega_rows, "team", onward)
    own, *weights = lax.optimization_barrier((omega_rows, *weights))
    last_step = team_count // 2
    gathered = []
    held = first
    for step in range(2, last_step):
        held = lax.ppermute(held, "team", onward)
        gathered.append((held, step))
    last_held = held
    held = own
    for step in range(1, team_count - last_step):
        held = lax.ppermute(held, "team", backward)
        gathered.append((held, -step))

    last_left = lax.ppermute(last_held[:, :cut], "team", onward)
    sources = [team_index, device_at(place - 1)]
    parts = products_of([own, first], sources)
    last_held, *parts = lax.optimization_barrier((last_held, *parts))
    last_right = lax.ppermute(last_held[:, cut:], "team", onward)
    for block, step in gathered:
        sources.append(device_at(place - step))
        parts += products_of([block], sources[-1:])
    sources.append(device_at(place - last_step))

    spots = [
        ((source // share_blocks) ^ rep_index) * share_blocks + source % share_blocks
        for source in sources
    ]
    row_spots = jnp.arange(rep_count * rows_share, dtype=jnp.int32) // block_rows
    masks = jnp.broadcast_to(
        (row_spots == spots[-1]).astype(jnp.int32).reshape(rep_count, rows_share, 1),
        (rep_count, rows_share, tile_width),
    )
    global_rows = rep_index * rows_share + jnp.arange(rows_share, dtype=jnp.int32)
    diagonal = (global_rows[:, None] == c_ids[None, :]).astype(jnp.int32)
    last_left, masks, diagonal = lax.optimization_barrier((last_left, masks, diagonal))
    shares = products_of([last_left], sources[-1:], spots, parts)
    kernel = functools.partial(last_kernel, cut)
    arrays = [masks, last_right, *weights, *shares]
    shares = call(kernel, rep_count, (rows_share, tile_width), [], arrays, 4 + rep_count)
    terms = [shares[0]]
    for flip in range(rep_count - 1, 0, -1):
        pairs = [(d, d ^ flip) for d in range(rep_count)]
        terms.append(lax.ppermute(shares[flip], "rep", pairs))
    arrays = [diagonal, *terms]
    return call(final_kernel, 1, (rows_share, tile_width), [], arrays, 2 + rep_count)[0]


def solution(mesh):
    in_specs = (P(("groups", "team"), "rep"), P("rep", ("groups", "team")), P(("groups", "team")))
    out_specs = P("rep", ("groups", "team"))
    return jax.shard_map(
        per_device, mesh=mesh, in_specs=in_specs, out_specs=out_specs, check_vma=False
    )
```

```python
import functools

import jax
import jax.numpy as jnp
from jax import lax
from jax.experimental import pallas as pl
from jax.experimental.pallas import tpu as pltpu
from jax.sharding import PartitionSpec as P

step_size = 0.5
penalty = 0.1
largest_bf16 = 3.3895313892515355e38


def halves(array):
    high = lax.reduce_precision(jnp.clip(array, -largest_bf16, largest_bf16), 8, 7)
    return high.astype(jnp.bfloat16), (array - high).astype(jnp.bfloat16)


def products(blocks, high, low, first_k=0):
    rows, depth = blocks[0].shape
    pieces = -(-depth // 2048)
    step = depth // pieces
    assert depth % pieces == 0 and step % 128 == 0
    all_rows = rows * len(blocks)
    total = jnp.zeros((all_rows, high.shape[1]), jnp.float32)
    for k in range(0, depth, step):
        values = jnp.concatenate([block[:, k : k + step] for block in blocks], 0)
        upper = jnp.clip(values, -largest_bf16, largest_bf16).astype(jnp.bfloat16)
        lower = (values - upper.astype(jnp.float32)).astype(jnp.bfloat16)
        both = jnp.concatenate([upper, lower], 0)
        span = slice(first_k + k, first_k + k + step)
        main = jnp.dot(both, high[span], preferred_element_type=jnp.float32)
        cross = jnp.dot(upper, low[span], preferred_element_type=jnp.float32)
        total += main[:all_rows] + main[all_rows:] + cross
    return [total[b * rows : (b + 1) * rows] for b in range(len(blocks))]


def slots_kernel(blocks_count, parts_count, places, *refs):
    blocks, refs = refs[:blocks_count], refs[blocks_count:]
    high, low, *refs = refs
    parts, outs = refs[:parts_count], refs[parts_count:]
    rows, columns = blocks[0].shape[0], high.shape[1]
    totals = products(blocks, high, low)
    start = pl.multiple_of(places[0], columns)
    ahead = lax.broadcasted_iota(jnp.int32, (rows, columns), 1)
    ahead -= lax.broadcasted_iota(jnp.int32, (rows, columns), 0)
    for b, block in enumerate(blocks):
        current = block[:, pl.ds(start, columns)]
        mask = ahead == places[1 + b]
        inverse = step_size / jnp.where(mask, current, 1.0)
        totals[b] += jnp.where(mask, inverse, 0.0)
    if len(outs) == blocks_count:
        for out, value in zip(outs, totals):
            out[...] = value
        return
    per_out = outs[0].shape[0] // rows
    for o, out in enumerate(outs):
        for b in range(per_out):
            found = jnp.zeros((rows, columns), jnp.float32)
            for position, value in enumerate([part[...] for part in parts] + totals):
                mine = places[1 + blocks_count + position] == o * per_out + b
                found = found + jnp.where(mine, value, 0.0)
            out[b * rows : (b + 1) * rows] = found


def last_kernel(first_k, masks, block, high, low, *refs):
    shares, outs = refs[: len(refs) // 2], refs[len(refs) // 2 :]
    rows = block.shape[0]
    (total,) = products([block], high, low, first_k)
    for o, out in enumerate(outs):
        for b in range(out.shape[0] // rows):
            span = slice(b * rows, (b + 1) * rows)
            out[span] = shares[o][span] + jnp.where(masks[o, span] != 0, total, 0.0)


def final_kernel(diagonal, *refs):
    *terms, out = refs
    moved = sum_of([term[...] for term in terms])
    limit = step_size * penalty
    shrunk = jnp.maximum(moved - limit, 0.0) + jnp.minimum(moved + limit, 0.0)
    out[...] = jnp.where(diagonal[...] != 0, moved, shrunk)


def call(kernel, count, shape, scalars, arrays, limit):
    return pl.pallas_call(
        kernel,
        out_shape=[jax.ShapeDtypeStruct(shape, jnp.float32)] * count,
        in_specs=[pl.BlockSpec(memory_space=pltpu.SMEM)] * len(scalars)
        + [pl.BlockSpec(memory_space=pltpu.VMEM)] * len(arrays),
        out_specs=[pl.BlockSpec(memory_space=pltpu.VMEM)] * count,
        compiler_params=pltpu.CompilerParams(vmem_limit_bytes=limit * 1024 * 1024),
        cost_estimate=pl.CostEstimate(
            flops=0, bytes_accessed=count * shape[0] * shape[1] * 4, transcendentals=0
        ),
    )(*scalars, *arrays)


def sum_of(terms):
    total = terms[0]
    for term in terms[1:]:
        total = total + term
    return total


def per_device(omega_rows, covariance_columns, tile_offsets):
    team_count = lax.axis_size("team")
    rep_count = lax.axis_size("rep")
    team_index = lax.axis_index("team")
    rep_index = lax.axis_index("rep")
    block_rows, part_width = omega_rows.shape
    tile_width = covariance_columns.shape[1]
    all_rows = block_rows * team_count
    rows_share = all_rows // rep_count
    offset = tile_offsets[0]
    assert all_rows <= part_width and part_width % tile_width == 0
    assert rows_share % block_rows == 0 and rep_count & (rep_count - 1) == 0 and rep_count > 1

    k_ids = rep_index * part_width + jnp.arange(part_width, dtype=jnp.int32)
    c_ids = offset + jnp.arange(tile_width, dtype=jnp.int32)
    chosen = (k_ids[:, None] == c_ids[None, :]).astype(jnp.float32)
    weights = halves(chosen - step_size * covariance_columns)

    cut = part_width // 4 * 3
    assert all_rows <= cut and cut % tile_width == 0

    share_blocks = rows_share // block_rows

    def products_of(blocks, sources, spots=(), parts=()):
        start = jnp.clip(offset, 0, cut - tile_width)
        shifts = [
            jnp.where(rep_index == 0, source * block_rows - offset, 1 << 20) for source in sources
        ]
        places = jnp.stack([start, *shifts, *spots]).astype(jnp.int32)
        count, rows = (rep_count, rows_share) if spots else (len(blocks), block_rows)
        kernel = functools.partial(slots_kernel, len(blocks), len(parts))
        arrays = [*blocks, *weights, *parts]
        return call(kernel, count, (rows, tile_width), [places], arrays, 4 + len(parts) // 4)

    ring = list(range(0, team_count, 2)) + list(range(1, team_count, 2))[::-1]
    onward = [(ring[k], ring[(k + 1) % team_count]) for k in range(team_count)]
    backward = [(to, source) for source, to in onward]
    rank = team_index // 2
    place = jnp.where(team_index % 2 == 0, rank, team_count - 1 - rank)

    def device_at(spot):
        spot = spot % team_count
        up = 2 * spot
        return jnp.where(up < team_count, up, 2 * team_count - 1 - up)

    first = lax.ppermute(omega_rows, "team", onward)
    own = omega_rows
    first, *weights = lax.optimization_barrier((first, *weights))
    last_step = team_count // 2
    gathered = []
    held = first
    for step in range(2, last_step):
        held = lax.ppermute(held, "team", onward)
        gathered.append((held, step))
    last_held = held
    held = own
    for step in range(1, team_count - last_step):
        held = lax.ppermute(held, "team", backward)
        gathered.append((held, -step))

    last_left = lax.ppermute(last_held[:, :cut], "team", onward)
    sources = [team_index, device_at(place - 1)]
    parts = products_of([own, first], sources)
    last_held, *parts = lax.optimization_barrier((last_held, *parts))
    last_right = lax.ppermute(last_held[:, cut:], "team", onward)
    for block, step in gathered:
        sources.append(device_at(place - step))
        parts += products_of([block], sources[-1:])
    sources.append(device_at(place - last_step))

    spots = [
        ((source // share_blocks) ^ rep_index) * share_blocks + source % share_blocks
        for source in sources
    ]
    row_spots = jnp.arange(rep_count * rows_share, dtype=jnp.int32) // block_rows
    masks = jnp.broadcast_to(
        (row_spots == spots[-1]).astype(jnp.int32).reshape(rep_count, rows_share, 1),
        (rep_count, rows_share, tile_width),
    )
    global_rows = rep_index * rows_share + jnp.arange(rows_share, dtype=jnp.int32)
    diagonal = (global_rows[:, None] == c_ids[None, :]).astype(jnp.int32)
    last_left, masks, diagonal = lax.optimization_barrier((last_left, masks, diagonal))
    shares = products_of([last_left], sources[-1:], spots, parts)
    kernel = functools.partial(last_kernel, cut)
    arrays = [masks, last_right, *weights, *shares]
    shares = call(kernel, rep_count, (rows_share, tile_width), [], arrays, 4 + rep_count)
    terms = [shares[0]]
    for flip in range(rep_count - 1, 0, -1):
        pairs = [(d, d ^ flip) for d in range(rep_count)]
        terms.append(lax.ppermute(shares[flip], "rep", pairs))
    arrays = [diagonal, *terms]
    return call(final_kernel, 1, (rows_share, tile_width), [], arrays, 2 + rep_count)[0]


def solution(mesh):
    in_specs = (P(("groups", "team"), "rep"), P("rep", ("groups", "team")), P(("groups", "team")))
    out_specs = P("rep", ("groups", "team"))
    return jax.shard_map(
        per_device, mesh=mesh, in_specs=in_specs, out_specs=out_specs, check_vma=False
    )
```

```python
import functools

import jax
import jax.numpy as jnp
from jax import lax
from jax.experimental import pallas as pl
from jax.experimental.pallas import tpu as pltpu
from jax.sharding import PartitionSpec as P

step_size = 0.5
penalty = 0.1
largest_bf16 = 3.3895313892515355e38


def halves(array):
    high = lax.reduce_precision(jnp.clip(array, -largest_bf16, largest_bf16), 8, 7)
    return high.astype(jnp.bfloat16), (array - high).astype(jnp.bfloat16)


def products(blocks, high, low, first_k=0):
    rows, depth = blocks[0].shape
    pieces = -(-depth // 2048)
    step = depth // pieces
    assert depth % pieces == 0 and step % 128 == 0
    all_rows = rows * len(blocks)
    total = jnp.zeros((all_rows, high.shape[1]), jnp.float32)
    for k in range(0, depth, step):
        values = jnp.concatenate([block[:, k : k + step] for block in blocks], 0)
        upper = jnp.clip(values, -largest_bf16, largest_bf16).astype(jnp.bfloat16)
        lower = (values - upper.astype(jnp.float32)).astype(jnp.bfloat16)
        both = jnp.concatenate([upper, lower], 0)
        span = slice(first_k + k, first_k + k + step)
        main = jnp.dot(both, high[span], preferred_element_type=jnp.float32)
        cross = jnp.dot(upper, low[span], preferred_element_type=jnp.float32)
        total += main[:all_rows] + main[all_rows:] + cross
    return [total[b * rows : (b + 1) * rows] for b in range(len(blocks))]


def slots_kernel(blocks_count, parts_count, places, *refs):
    blocks, refs = refs[:blocks_count], refs[blocks_count:]
    high, low, *refs = refs
    parts, outs = refs[:parts_count], refs[parts_count:]
    rows, columns = blocks[0].shape[0], high.shape[1]
    totals = products(blocks, high, low)
    start = pl.multiple_of(places[0], columns)
    ahead = lax.broadcasted_iota(jnp.int32, (rows, columns), 1)
    ahead -= lax.broadcasted_iota(jnp.int32, (rows, columns), 0)
    for b, block in enumerate(blocks):
        current = block[:, pl.ds(start, columns)]
        mask = ahead == places[1 + b]
        inverse = step_size / jnp.where(mask, current, 1.0)
        totals[b] += jnp.where(mask, inverse, 0.0)
    if len(outs) == blocks_count:
        for out, value in zip(outs, totals):
            out[...] = value
        return
    per_out = outs[0].shape[0] // rows
    for o, out in enumerate(outs):
        for b in range(per_out):
            found = jnp.zeros((rows, columns), jnp.float32)
            for position, value in enumerate([part[...] for part in parts] + totals):
                mine = places[1 + blocks_count + position] == o * per_out + b
                found = found + jnp.where(mine, value, 0.0)
            out[b * rows : (b + 1) * rows] = found


def last_kernel(first_k, masks, block, high, low, *refs):
    shares, outs = refs[: len(refs) // 2], refs[len(refs) // 2 :]
    rows = block.shape[0]
    (total,) = products([block], high, low, first_k)
    for o, out in enumerate(outs):
        for b in range(out.shape[0] // rows):
            span = slice(b * rows, (b + 1) * rows)
            out[span] = shares[o][span] + jnp.where(masks[o, span] != 0, total, 0.0)


def final_kernel(diagonal, *refs):
    *terms, out = refs
    moved = sum_of([term[...] for term in terms])
    limit = step_size * penalty
    shrunk = jnp.maximum(moved - limit, 0.0) + jnp.minimum(moved + limit, 0.0)
    out[...] = jnp.where(diagonal[...] != 0, moved, shrunk)


def call(kernel, count, shape, scalars, arrays, limit):
    return pl.pallas_call(
        kernel,
        out_shape=[jax.ShapeDtypeStruct(shape, jnp.float32)] * count,
        in_specs=[pl.BlockSpec(memory_space=pltpu.SMEM)] * len(scalars)
        + [pl.BlockSpec(memory_space=pltpu.VMEM)] * len(arrays),
        out_specs=[pl.BlockSpec(memory_space=pltpu.VMEM)] * count,
        compiler_params=pltpu.CompilerParams(vmem_limit_bytes=limit * 1024 * 1024),
        cost_estimate=pl.CostEstimate(
            flops=0, bytes_accessed=count * shape[0] * shape[1] * 4, transcendentals=0
        ),
    )(*scalars, *arrays)


def sum_of(terms):
    total = terms[0]
    for term in terms[1:]:
        total = total + term
    return total


def per_device(omega_rows, covariance_columns, tile_offsets):
    team_count = lax.axis_size("team")
    rep_count = lax.axis_size("rep")
    team_index = lax.axis_index("team")
    rep_index = lax.axis_index("rep")
    block_rows, part_width = omega_rows.shape
    tile_width = covariance_columns.shape[1]
    all_rows = block_rows * team_count
    rows_share = all_rows // rep_count
    offset = tile_offsets[0]
    assert all_rows <= part_width and part_width % tile_width == 0
    assert rows_share % block_rows == 0 and rep_count & (rep_count - 1) == 0 and rep_count > 1

    k_ids = rep_index * part_width + jnp.arange(part_width, dtype=jnp.int32)
    c_ids = offset + jnp.arange(tile_width, dtype=jnp.int32)
    chosen = (k_ids[:, None] == c_ids[None, :]).astype(jnp.float32)
    weights = halves(chosen - step_size * covariance_columns)

    cut = part_width // 4 * 3
    assert all_rows <= cut and cut % tile_width == 0

    share_blocks = rows_share // block_rows

    def products_of(blocks, sources, spots=(), parts=()):
        start = jnp.clip(offset, 0, cut - tile_width)
        shifts = [
            jnp.where(rep_index == 0, source * block_rows - offset, 1 << 20) for source in sources
        ]
        places = jnp.stack([start, *shifts, *spots]).astype(jnp.int32)
        count, rows = (rep_count, rows_share) if spots else (len(blocks), block_rows)
        kernel = functools.partial(slots_kernel, len(blocks), len(parts))
        arrays = [*blocks, *weights, *parts]
        return call(kernel, count, (rows, tile_width), [places], arrays, 4 + len(parts) // 4)

    ring = list(range(0, team_count, 2)) + list(range(1, team_count, 2))[::-1]
    onward = [(ring[k], ring[(k + 1) % team_count]) for k in range(team_count)]
    backward = [(to, source) for source, to in onward]
    rank = team_index // 2
    place = jnp.where(team_index % 2 == 0, rank, team_count - 1 - rank)

    def device_at(spot):
        spot = spot % team_count
        up = 2 * spot
        return jnp.where(up < team_count, up, 2 * team_count - 1 - up)

    first = lax.ppermute(omega_rows, "team", onward)
    own = omega_rows
    first, *weights = lax.optimization_barrier((first, *weights))
    last_step = team_count // 2
    gathered = []
    held = first
    for step in range(2, last_step):
        held = lax.ppermute(held, "team", onward)
        gathered.append((held, step))
    last_held = held
    held = own
    for step in range(1, team_count - last_step):
        held = lax.ppermute(held, "team", backward)
        gathered.append((held, -step))

    last_left = lax.ppermute(last_held[:, :cut], "team", onward)
    sources = [team_index, device_at(place - 1)]
    parts = products_of([own, first], sources)
    last_held, *parts = lax.optimization_barrier((last_held, *parts))
    last_right = lax.ppermute(last_held[:, cut:], "team", onward)
    for block, step in gathered:
        sources.append(device_at(place - step))
        parts += products_of([block], sources[-1:])
    sources.append(device_at(place - last_step))

    spots = [
        ((source // share_blocks) ^ rep_index) * share_blocks + source % share_blocks
        for source in sources
    ]
    row_spots = jnp.arange(rep_count * rows_share, dtype=jnp.int32) // block_rows
    masks = jnp.broadcast_to(
        (row_spots == spots[-1]).astype(jnp.int32).reshape(rep_count, rows_share, 1),
        (rep_count, rows_share, tile_width),
    )
    global_rows = rep_index * rows_share + jnp.arange(rows_share, dtype=jnp.int32)
    diagonal = (global_rows[:, None] == c_ids[None, :]).astype(jnp.int32)
    last_left, masks, diagonal = lax.optimization_barrier((last_left, masks, diagonal))
    shares = products_of([last_left], sources[-1:], spots, parts)
    kernel = functools.partial(last_kernel, cut)
    arrays = [masks, last_right, *weights, *shares]
    shares = call(kernel, rep_count, (rows_share, tile_width), [], arrays, 4 + rep_count)
    terms = [shares[0]]
    middle = rep_count // 2
    for flip in [*range(middle, rep_count), *range(middle - 1, 0, -1)]:
        pairs = [(d, d ^ flip) for d in range(rep_count)]
        terms.append(lax.ppermute(shares[flip], "rep", pairs))
    arrays = [diagonal, *terms]
    return call(final_kernel, 1, (rows_share, tile_width), [], arrays, 2 + rep_count)[0]


def solution(mesh):
    in_specs = (P(("groups", "team"), "rep"), P("rep", ("groups", "team")), P(("groups", "team")))
    out_specs = P("rep", ("groups", "team"))
    return jax.shard_map(
        per_device, mesh=mesh, in_specs=in_specs, out_specs=out_specs, check_vma=False
    )
```

```python
import functools

import jax
import jax.numpy as jnp
from jax import lax
from jax.experimental import pallas as pl
from jax.experimental.pallas import tpu as pltpu
from jax.sharding import PartitionSpec as P

step_size = 0.5
penalty = 0.1
largest_bf16 = 3.3895313892515355e38


def halves(array):
    high = lax.reduce_precision(jnp.clip(array, -largest_bf16, largest_bf16), 8, 7)
    return high.astype(jnp.bfloat16), (array - high).astype(jnp.bfloat16)


def products(blocks, high, low, first_k=0):
    rows, depth = blocks[0].shape
    pieces = -(-depth // 2048)
    step = depth // pieces
    assert depth % pieces == 0 and step % 128 == 0
    all_rows = rows * len(blocks)
    total = jnp.zeros((all_rows, high.shape[1]), jnp.float32)
    for k in range(0, depth, step):
        values = jnp.concatenate([block[:, k : k + step] for block in blocks], 0)
        upper = jnp.clip(values, -largest_bf16, largest_bf16).astype(jnp.bfloat16)
        lower = (values - upper.astype(jnp.float32)).astype(jnp.bfloat16)
        both = jnp.concatenate([upper, lower], 0)
        span = slice(first_k + k, first_k + k + step)
        main = jnp.dot(both, high[span], preferred_element_type=jnp.float32)
        cross = jnp.dot(upper, low[span], preferred_element_type=jnp.float32)
        total += main[:all_rows] + main[all_rows:] + cross
    return [total[b * rows : (b + 1) * rows] for b in range(len(blocks))]


def slots_kernel(blocks_count, parts_count, places, *refs):
    blocks, refs = refs[:blocks_count], refs[blocks_count:]
    high, low, *refs = refs
    parts, outs = refs[:parts_count], refs[parts_count:]
    rows, columns = blocks[0].shape[0], high.shape[1]
    totals = products(blocks, high, low)
    start = pl.multiple_of(places[0], columns)
    ahead = lax.broadcasted_iota(jnp.int32, (rows, columns), 1)
    ahead -= lax.broadcasted_iota(jnp.int32, (rows, columns), 0)
    for b, block in enumerate(blocks):
        current = block[:, pl.ds(start, columns)]
        mask = ahead == places[1 + b]
        inverse = step_size / jnp.where(mask, current, 1.0)
        totals[b] += jnp.where(mask, inverse, 0.0)
    if len(outs) == blocks_count:
        for out, value in zip(outs, totals):
            out[...] = value
        return
    per_out = outs[0].shape[0] // rows
    for o, out in enumerate(outs):
        for b in range(per_out):
            found = jnp.zeros((rows, columns), jnp.float32)
            for position, value in enumerate([part[...] for part in parts] + totals):
                mine = places[1 + blocks_count + position] == o * per_out + b
                found = found + jnp.where(mine, value, 0.0)
            out[b * rows : (b + 1) * rows] = found


def last_kernel(first_k, masks, block, high, low, *refs):
    shares, outs = refs[: len(refs) // 2], refs[len(refs) // 2 :]
    rows = block.shape[0]
    (total,) = products([block], high, low, first_k)
    for o, out in enumerate(outs):
        for b in range(out.shape[0] // rows):
            span = slice(b * rows, (b + 1) * rows)
            out[span] = shares[o][span] + jnp.where(masks[o, span] != 0, total, 0.0)


def final_kernel(diagonal, *refs):
    *terms, out = refs
    moved = sum_of([term[...] for term in terms])
    limit = step_size * penalty
    shrunk = jnp.maximum(moved - limit, 0.0) + jnp.minimum(moved + limit, 0.0)
    out[...] = jnp.where(diagonal[...] != 0, moved, shrunk)


def call(kernel, count, shape, scalars, arrays, limit):
    return pl.pallas_call(
        kernel,
        out_shape=[jax.ShapeDtypeStruct(shape, jnp.float32)] * count,
        in_specs=[pl.BlockSpec(memory_space=pltpu.SMEM)] * len(scalars)
        + [pl.BlockSpec(memory_space=pltpu.VMEM)] * len(arrays),
        out_specs=[pl.BlockSpec(memory_space=pltpu.VMEM)] * count,
        compiler_params=pltpu.CompilerParams(vmem_limit_bytes=limit * 1024 * 1024),
        cost_estimate=pl.CostEstimate(
            flops=0, bytes_accessed=count * shape[0] * shape[1] * 4, transcendentals=0
        ),
    )(*scalars, *arrays)


def sum_of(terms):
    total = terms[0]
    for term in terms[1:]:
        total = total + term
    return total


def per_device(omega_rows, covariance_columns, tile_offsets):
    team_count = lax.axis_size("team")
    rep_count = lax.axis_size("rep")
    team_index = lax.axis_index("team")
    rep_index = lax.axis_index("rep")
    block_rows, part_width = omega_rows.shape
    tile_width = covariance_columns.shape[1]
    all_rows = block_rows * team_count
    rows_share = all_rows // rep_count
    offset = tile_offsets[0]
    assert all_rows <= part_width and part_width % tile_width == 0
    assert rows_share % block_rows == 0 and rep_count & (rep_count - 1) == 0 and rep_count > 1

    k_ids = rep_index * part_width + jnp.arange(part_width, dtype=jnp.int32)
    c_ids = offset + jnp.arange(tile_width, dtype=jnp.int32)
    chosen = (k_ids[:, None] == c_ids[None, :]).astype(jnp.float32)
    weights = halves(chosen - step_size * covariance_columns)

    cut = part_width // 4 * 3
    assert all_rows <= cut and cut % tile_width == 0

    share_blocks = rows_share // block_rows

    def products_of(blocks, sources, spots=(), parts=()):
        start = jnp.clip(offset, 0, cut - tile_width)
        shifts = [
            jnp.where(rep_index == 0, source * block_rows - offset, 1 << 20) for source in sources
        ]
        places = jnp.stack([start, *shifts, *spots]).astype(jnp.int32)
        count, rows = (rep_count, rows_share) if spots else (len(blocks), block_rows)
        kernel = functools.partial(slots_kernel, len(blocks), len(parts))
        arrays = [*blocks, *weights, *parts]
        return call(kernel, count, (rows, tile_width), [places], arrays, 4 + len(parts) // 4)

    ring = list(range(0, team_count, 2)) + list(range(1, team_count, 2))[::-1]
    onward = [(ring[k], ring[(k + 1) % team_count]) for k in range(team_count)]
    backward = [(to, source) for source, to in onward]
    rank = team_index // 2
    place = jnp.where(team_index % 2 == 0, rank, team_count - 1 - rank)

    def device_at(spot):
        spot = spot % team_count
        up = 2 * spot
        return jnp.where(up < team_count, up, 2 * team_count - 1 - up)

    first = lax.ppermute(omega_rows, "team", onward)
    own = omega_rows
    first, *weights = lax.optimization_barrier((first, *weights))
    last_step = team_count // 2
    gathered = []
    held = first
    for step in range(2, last_step):
        held = lax.ppermute(held, "team", onward)
        gathered.append((held, step))
    last_held = held
    held = own
    for step in range(1, team_count - last_step):
        held = lax.ppermute(held, "team", backward)
        gathered.append((held, -step))

    last_left = lax.ppermute(last_held[:, :cut], "team", onward)
    last_right = lax.ppermute(last_held[:, cut:], "team", onward)
    sources = [team_index, device_at(place - 1)]
    parts = products_of([own, first], sources)
    for block, step in gathered:
        sources.append(device_at(place - step))
        parts += products_of([block], sources[-1:])
    sources.append(device_at(place - last_step))

    spots = [
        ((source // share_blocks) ^ rep_index) * share_blocks + source % share_blocks
        for source in sources
    ]
    row_spots = jnp.arange(rep_count * rows_share, dtype=jnp.int32) // block_rows
    masks = jnp.broadcast_to(
        (row_spots == spots[-1]).astype(jnp.int32).reshape(rep_count, rows_share, 1),
        (rep_count, rows_share, tile_width),
    )
    global_rows = rep_index * rows_share + jnp.arange(rows_share, dtype=jnp.int32)
    diagonal = (global_rows[:, None] == c_ids[None, :]).astype(jnp.int32)
    last_left, masks, diagonal = lax.optimization_barrier((last_left, masks, diagonal))
    shares = products_of([last_left], sources[-1:], spots, parts)
    kernel = functools.partial(last_kernel, cut)
    arrays = [masks, last_right, *weights, *shares]
    shares = call(kernel, rep_count, (rows_share, tile_width), [], arrays, 4 + rep_count)
    terms = [shares[0]]
    for flip in range(rep_count - 1, 0, -1):
        pairs = [(d, d ^ flip) for d in range(rep_count)]
        terms.append(lax.ppermute(shares[flip], "rep", pairs))
    arrays = [diagonal, *terms]
    return call(final_kernel, 1, (rows_share, tile_width), [], arrays, 2 + rep_count)[0]


def solution(mesh):
    in_specs = (P(("groups", "team"), "rep"), P("rep", ("groups", "team")), P(("groups", "team")))
    out_specs = P("rep", ("groups", "team"))
    return jax.shard_map(
        per_device, mesh=mesh, in_specs=in_specs, out_specs=out_specs, check_vma=False
    )
```

```python
import functools

import jax
import jax.numpy as jnp
from jax import lax
from jax.experimental import pallas as pl
from jax.experimental.pallas import tpu as pltpu
from jax.sharding import PartitionSpec as P

step_size = 0.5
penalty = 0.1
largest_bf16 = 3.3895313892515355e38


def halves(array):
    high = lax.reduce_precision(jnp.clip(array, -largest_bf16, largest_bf16), 8, 7)
    return high.astype(jnp.bfloat16), (array - high).astype(jnp.bfloat16)


def products(blocks, high, low, first_k=0):
    rows, depth = blocks[0].shape
    pieces = -(-depth // 2048)
    step = depth // pieces
    assert depth % pieces == 0 and step % 128 == 0
    all_rows = rows * len(blocks)
    total = jnp.zeros((all_rows, high.shape[1]), jnp.float32)
    for k in range(0, depth, step):
        values = jnp.concatenate([block[:, k : k + step] for block in blocks], 0)
        upper = jnp.clip(values, -largest_bf16, largest_bf16).astype(jnp.bfloat16)
        lower = (values - upper.astype(jnp.float32)).astype(jnp.bfloat16)
        both = jnp.concatenate([upper, lower], 0)
        span = slice(first_k + k, first_k + k + step)
        main = jnp.dot(both, high[span], preferred_element_type=jnp.float32)
        cross = jnp.dot(upper, low[span], preferred_element_type=jnp.float32)
        total += main[:all_rows] + main[all_rows:] + cross
    return [total[b * rows : (b + 1) * rows] for b in range(len(blocks))]


def slots_kernel(blocks_count, parts_count, places, *refs):
    blocks, refs = refs[:blocks_count], refs[blocks_count:]
    high, low, *refs = refs
    parts, outs = refs[:parts_count], refs[parts_count:]
    rows, columns = blocks[0].shape[0], high.shape[1]
    totals = products(blocks, high, low)
    start = pl.multiple_of(places[0], columns)
    ahead = lax.broadcasted_iota(jnp.int32, (rows, columns), 1)
    ahead -= lax.broadcasted_iota(jnp.int32, (rows, columns), 0)
    for b, block in enumerate(blocks):
        current = block[:, pl.ds(start, columns)]
        mask = ahead == places[1 + b]
        inverse = step_size / jnp.where(mask, current, 1.0)
        totals[b] += jnp.where(mask, inverse, 0.0)
    if len(outs) == blocks_count:
        for out, value in zip(outs, totals):
            out[...] = value
        return
    per_out = outs[0].shape[0] // rows
    for o, out in enumerate(outs):
        for b in range(per_out):
            found = jnp.zeros((rows, columns), jnp.float32)
            for position, value in enumerate([part[...] for part in parts] + totals):
                mine = places[1 + blocks_count + position] == o * per_out + b
                found = found + jnp.where(mine, value, 0.0)
            out[b * rows : (b + 1) * rows] = found


def last_kernel(first_k, masks, block, high, low, *refs):
    shares, outs = refs[: len(refs) // 2], refs[len(refs) // 2 :]
    rows = block.shape[0]
    (total,) = products([block], high, low, first_k)
    for o, out in enumerate(outs):
        for b in range(out.shape[0] // rows):
            span = slice(b * rows, (b + 1) * rows)
            out[span] = shares[o][span] + jnp.where(masks[o, span] != 0, total, 0.0)


def final_kernel(diagonal, *refs):
    *terms, out = refs
    moved = sum_of([term[...] for term in terms])
    limit = step_size * penalty
    shrunk = jnp.maximum(moved - limit, 0.0) + jnp.minimum(moved + limit, 0.0)
    out[...] = jnp.where(diagonal[...] != 0, moved, shrunk)


def call(kernel, count, shape, scalars, arrays, limit):
    return pl.pallas_call(
        kernel,
        out_shape=[jax.ShapeDtypeStruct(shape, jnp.float32)] * count,
        in_specs=[pl.BlockSpec(memory_space=pltpu.SMEM)] * len(scalars)
        + [pl.BlockSpec(memory_space=pltpu.VMEM)] * len(arrays),
        out_specs=[pl.BlockSpec(memory_space=pltpu.VMEM)] * count,
        compiler_params=pltpu.CompilerParams(vmem_limit_bytes=limit * 1024 * 1024),
        cost_estimate=pl.CostEstimate(
            flops=0, bytes_accessed=count * shape[0] * shape[1] * 4, transcendentals=0
        ),
    )(*scalars, *arrays)


def sum_of(terms):
    total = terms[0]
    for term in terms[1:]:
        total = total + term
    return total


def per_device(omega_rows, covariance_columns, tile_offsets):
    team_count = lax.axis_size("team")
    rep_count = lax.axis_size("rep")
    team_index = lax.axis_index("team")
    rep_index = lax.axis_index("rep")
    block_rows, part_width = omega_rows.shape
    tile_width = covariance_columns.shape[1]
    all_rows = block_rows * team_count
    rows_share = all_rows // rep_count
    offset = tile_offsets[0]
    assert all_rows <= part_width and part_width % tile_width == 0
    assert rows_share % block_rows == 0 and rep_count & (rep_count - 1) == 0 and rep_count > 1

    k_ids = rep_index * part_width + jnp.arange(part_width, dtype=jnp.int32)
    c_ids = offset + jnp.arange(tile_width, dtype=jnp.int32)
    chosen = (k_ids[:, None] == c_ids[None, :]).astype(jnp.float32)
    weights = halves(chosen - step_size * covariance_columns)

    cut = part_width // 16 * 13
    assert all_rows <= cut and cut % tile_width == 0

    share_blocks = rows_share // block_rows

    def products_of(blocks, sources, spots=(), parts=()):
        start = jnp.clip(offset, 0, cut - tile_width)
        shifts = [
            jnp.where(rep_index == 0, source * block_rows - offset, 1 << 20) for source in sources
        ]
        places = jnp.stack([start, *shifts, *spots]).astype(jnp.int32)
        count, rows = (rep_count, rows_share) if spots else (len(blocks), block_rows)
        kernel = functools.partial(slots_kernel, len(blocks), len(parts))
        arrays = [*blocks, *weights, *parts]
        return call(kernel, count, (rows, tile_width), [places], arrays, 4 + len(parts) // 4)

    ring = list(range(0, team_count, 2)) + list(range(1, team_count, 2))[::-1]
    onward = [(ring[k], ring[(k + 1) % team_count]) for k in range(team_count)]
    backward = [(to, source) for source, to in onward]
    rank = team_index // 2
    place = jnp.where(team_index % 2 == 0, rank, team_count - 1 - rank)

    def device_at(spot):
        spot = spot % team_count
        up = 2 * spot
        return jnp.where(up < team_count, up, 2 * team_count - 1 - up)

    first = lax.ppermute(omega_rows, "team", onward)
    own = omega_rows
    first, *weights = lax.optimization_barrier((first, *weights))
    last_step = team_count // 2
    gathered = []
    held = first
    for step in range(2, last_step):
        held = lax.ppermute(held, "team", onward)
        gathered.append((held, step))
    last_held = held
    held = own
    for step in range(1, team_count - last_step):
        held = lax.ppermute(held, "team", backward)
        gathered.append((held, -step))

    last_left = lax.ppermute(last_held[:, :cut], "team", onward)
    last_right = lax.ppermute(last_held[:, cut:], "team", onward)
    sources = [team_index, device_at(place - 1)]
    parts = products_of([own, first], sources)
    for block, step in gathered:
        sources.append(device_at(place - step))
        parts += products_of([block], sources[-1:])
    sources.append(device_at(place - last_step))

    spots = [
        ((source // share_blocks) ^ rep_index) * share_blocks + source % share_blocks
        for source in sources
    ]
    row_spots = jnp.arange(rep_count * rows_share, dtype=jnp.int32) // block_rows
    masks = jnp.broadcast_to(
        (row_spots == spots[-1]).astype(jnp.int32).reshape(rep_count, rows_share, 1),
        (rep_count, rows_share, tile_width),
    )
    global_rows = rep_index * rows_share + jnp.arange(rows_share, dtype=jnp.int32)
    diagonal = (global_rows[:, None] == c_ids[None, :]).astype(jnp.int32)
    last_left, masks, diagonal = lax.optimization_barrier((last_left, masks, diagonal))
    shares = products_of([last_left], sources[-1:], spots, parts)
    kernel = functools.partial(last_kernel, cut)
    arrays = [masks, last_right, *weights, *shares]
    shares = call(kernel, rep_count, (rows_share, tile_width), [], arrays, 4 + rep_count)
    terms = [shares[0]]
    for flip in range(rep_count - 1, 0, -1):
        pairs = [(d, d ^ flip) for d in range(rep_count)]
        terms.append(lax.ppermute(shares[flip], "rep", pairs))
    arrays = [diagonal, *terms]
    return call(final_kernel, 1, (rows_share, tile_width), [], arrays, 2 + rep_count)[0]


def solution(mesh):
    in_specs = (P(("groups", "team"), "rep"), P("rep", ("groups", "team")), P(("groups", "team")))
    out_specs = P("rep", ("groups", "team"))
    return jax.shard_map(
        per_device, mesh=mesh, in_specs=in_specs, out_specs=out_specs, check_vma=False
    )
```

```python
import functools

import jax
import jax.numpy as jnp
from jax import lax
from jax.experimental import pallas as pl
from jax.experimental.pallas import tpu as pltpu
from jax.sharding import PartitionSpec as P

step_size = 0.5
penalty = 0.1
largest_bf16 = 3.3895313892515355e38


def halves(array):
    high = lax.reduce_precision(jnp.clip(array, -largest_bf16, largest_bf16), 8, 7)
    return high.astype(jnp.bfloat16), (array - high).astype(jnp.bfloat16)


def products(blocks, high, low, first_k=0):
    rows, depth = blocks[0].shape
    pieces = -(-depth // 2048)
    step = depth // pieces
    assert depth % pieces == 0 and step % 128 == 0
    all_rows = rows * len(blocks)
    total = jnp.zeros((all_rows, high.shape[1]), jnp.float32)
    for k in range(0, depth, step):
        values = jnp.concatenate([block[:, k : k + step] for block in blocks], 0)
        upper = jnp.clip(values, -largest_bf16, largest_bf16).astype(jnp.bfloat16)
        lower = (values - upper.astype(jnp.float32)).astype(jnp.bfloat16)
        both = jnp.concatenate([upper, lower], 0)
        span = slice(first_k + k, first_k + k + step)
        main = jnp.dot(both, high[span], preferred_element_type=jnp.float32)
        cross = jnp.dot(upper, low[span], preferred_element_type=jnp.float32)
        total += main[:all_rows] + main[all_rows:] + cross
    return [total[b * rows : (b + 1) * rows] for b in range(len(blocks))]


def slots_kernel(blocks_count, parts_count, places, *refs):
    blocks, refs = refs[:blocks_count], refs[blocks_count:]
    high, low, *refs = refs
    parts, outs = refs[:parts_count], refs[parts_count:]
    rows, columns = blocks[0].shape[0], high.shape[1]
    totals = products(blocks, high, low)
    start = pl.multiple_of(places[0], columns)
    ahead = lax.broadcasted_iota(jnp.int32, (rows, columns), 1)
    ahead -= lax.broadcasted_iota(jnp.int32, (rows, columns), 0)
    for b, block in enumerate(blocks):
        current = block[:, pl.ds(start, columns)]
        mask = ahead == places[1 + b]
        inverse = step_size / jnp.where(mask, current, 1.0)
        totals[b] += jnp.where(mask, inverse, 0.0)
    if len(outs) == blocks_count:
        for out, value in zip(outs, totals):
            out[...] = value
        return
    per_out = outs[0].shape[0] // rows
    for o, out in enumerate(outs):
        for b in range(per_out):
            found = jnp.zeros((rows, columns), jnp.float32)
            for position, value in enumerate([part[...] for part in parts] + totals):
                mine = places[1 + blocks_count + position] == o * per_out + b
                found = found + jnp.where(mine, value, 0.0)
            out[b * rows : (b + 1) * rows] = found


def last_kernel(first_k, masks, block, high, low, *refs):
    shares, outs = refs[: len(refs) // 2], refs[len(refs) // 2 :]
    rows = block.shape[0]
    (total,) = products([block], high, low, first_k)
    for o, out in enumerate(outs):
        for b in range(out.shape[0] // rows):
            span = slice(b * rows, (b + 1) * rows)
            out[span] = shares[o][span] + jnp.where(masks[o, span] != 0, total, 0.0)


def final_kernel(diagonal, *refs):
    *terms, out = refs
    moved = sum_of([term[...] for term in terms])
    limit = step_size * penalty
    shrunk = jnp.maximum(moved - limit, 0.0) + jnp.minimum(moved + limit, 0.0)
    out[...] = jnp.where(diagonal[...] != 0, moved, shrunk)


def call(kernel, count, shape, scalars, arrays, limit):
    return pl.pallas_call(
        kernel,
        out_shape=[jax.ShapeDtypeStruct(shape, jnp.float32)] * count,
        in_specs=[pl.BlockSpec(memory_space=pltpu.SMEM)] * len(scalars)
        + [pl.BlockSpec(memory_space=pltpu.VMEM)] * len(arrays),
        out_specs=[pl.BlockSpec(memory_space=pltpu.VMEM)] * count,
        compiler_params=pltpu.CompilerParams(vmem_limit_bytes=limit * 1024 * 1024),
        cost_estimate=pl.CostEstimate(
            flops=0, bytes_accessed=count * shape[0] * shape[1] * 4, transcendentals=0
        ),
    )(*scalars, *arrays)


def sum_of(terms):
    total = terms[0]
    for term in terms[1:]:
        total = total + term
    return total


def per_device(omega_rows, covariance_columns, tile_offsets):
    team_count = lax.axis_size("team")
    rep_count = lax.axis_size("rep")
    team_index = lax.axis_index("team")
    rep_index = lax.axis_index("rep")
    block_rows, part_width = omega_rows.shape
    tile_width = covariance_columns.shape[1]
    all_rows = block_rows * team_count
    rows_share = all_rows // rep_count
    offset = tile_offsets[0]
    assert all_rows <= part_width and part_width % tile_width == 0
    assert rows_share % block_rows == 0 and rep_count & (rep_count - 1) == 0 and rep_count > 1

    k_ids = rep_index * part_width + jnp.arange(part_width, dtype=jnp.int32)
    c_ids = offset + jnp.arange(tile_width, dtype=jnp.int32)
    chosen = (k_ids[:, None] == c_ids[None, :]).astype(jnp.float32)
    weights = halves(chosen - step_size * covariance_columns)

    cut = part_width // 4 * 3
    assert all_rows <= cut and cut % tile_width == 0

    share_blocks = rows_share // block_rows

    def products_of(blocks, sources, spots=(), parts=()):
        start = jnp.clip(offset, 0, cut - tile_width)
        shifts = [
            jnp.where(rep_index == 0, source * block_rows - offset, 1 << 20) for source in sources
        ]
        places = jnp.stack([start, *shifts, *spots]).astype(jnp.int32)
        count, rows = (rep_count, rows_share) if spots else (len(blocks), block_rows)
        kernel = functools.partial(slots_kernel, len(blocks), len(parts))
        arrays = [*blocks, *weights, *parts]
        return call(kernel, count, (rows, tile_width), [places], arrays, 4 + len(parts) // 4)

    ring = list(range(0, team_count, 2)) + list(range(1, team_count, 2))[::-1]
    onward = [(ring[k], ring[(k + 1) % team_count]) for k in range(team_count)]
    backward = [(to, source) for source, to in onward]
    rank = team_index // 2
    place = jnp.where(team_index % 2 == 0, rank, team_count - 1 - rank)

    def device_at(spot):
        spot = spot % team_count
        up = 2 * spot
        return jnp.where(up < team_count, up, 2 * team_count - 1 - up)

    first = lax.ppermute(omega_rows, "team", onward)
    own = omega_rows
    first, *weights = lax.optimization_barrier((first, *weights))
    last_step = team_count // 2
    gathered = []
    held = first
    for step in range(2, last_step):
        held = lax.ppermute(held, "team", onward)
        gathered.append((held, step))
    last_held = held
    held = own
    for step in range(1, team_count - last_step):
        held = lax.ppermute(held, "team", backward)
        gathered.append((held, -step))

    last_left = lax.ppermute(last_held[:, :cut], "team", onward)
    last_right = lax.ppermute(last_held[:, cut:], "team", onward)
    sources = [team_index, device_at(place - 1)]
    parts = products_of([own, first], sources)
    for block, step in gathered:
        sources.append(device_at(place - step))
        parts += products_of([block], sources[-1:])
    sources.append(device_at(place - last_step))

    spots = [
        ((source // share_blocks) ^ rep_index) * share_blocks + source % share_blocks
        for source in sources
    ]
    row_spots = jnp.arange(rep_count * rows_share, dtype=jnp.int32) // block_rows
    masks = jnp.broadcast_to(
        (row_spots == spots[-1]).astype(jnp.int32).reshape(rep_count, rows_share, 1),
        (rep_count, rows_share, tile_width),
    )
    global_rows = rep_index * rows_share + jnp.arange(rows_share, dtype=jnp.int32)
    diagonal = (global_rows[:, None] == c_ids[None, :]).astype(jnp.int32)
    last_left, masks, diagonal = lax.optimization_barrier((last_left, masks, diagonal))
    shares = products_of([last_left], sources[-1:], spots, parts)
    kernel = functools.partial(last_kernel, cut)
    arrays = [masks, last_right, *weights, *shares]
    shares = call(kernel, rep_count, (rows_share, tile_width), [], arrays, 4 + rep_count)
    terms = [shares[0]]
    middle = rep_count // 2
    for flip in [*range(middle, rep_count), *range(middle - 1, 0, -1)]:
        pairs = [(d, d ^ flip) for d in range(rep_count)]
        terms.append(lax.ppermute(shares[flip], "rep", pairs))
    arrays = [diagonal, *terms]
    return call(final_kernel, 1, (rows_share, tile_width), [], arrays, 2 + rep_count)[0]


def solution(mesh):
    in_specs = (P(("groups", "team"), "rep"), P("rep", ("groups", "team")), P(("groups", "team")))
    out_specs = P("rep", ("groups", "team"))
    return jax.shard_map(
        per_device, mesh=mesh, in_specs=in_specs, out_specs=out_specs, check_vma=False
    )
```

```python
import functools

import jax
import jax.numpy as jnp
from jax import lax
from jax.experimental import pallas as pl
from jax.experimental.pallas import tpu as pltpu
from jax.sharding import PartitionSpec as P

step_size = 0.5
penalty = 0.1
largest_bf16 = 3.3895313892515355e38


def halves(array):
    high = lax.reduce_precision(jnp.clip(array, -largest_bf16, largest_bf16), 8, 7)
    return high.astype(jnp.bfloat16), (array - high).astype(jnp.bfloat16)


def products(blocks, high, low, first_k=0):
    rows, depth = blocks[0].shape
    pieces = -(-depth // 2048)
    step = depth // pieces
    assert depth % pieces == 0 and step % 128 == 0
    all_rows = rows * len(blocks)
    total = jnp.zeros((all_rows, high.shape[1]), jnp.float32)
    for k in range(0, depth, step):
        values = jnp.concatenate([block[:, k : k + step] for block in blocks], 0)
        upper = jnp.clip(values, -largest_bf16, largest_bf16).astype(jnp.bfloat16)
        lower = (values - upper.astype(jnp.float32)).astype(jnp.bfloat16)
        both = jnp.concatenate([upper, lower], 0)
        span = slice(first_k + k, first_k + k + step)
        main = jnp.dot(both, high[span], preferred_element_type=jnp.float32)
        cross = jnp.dot(upper, low[span], preferred_element_type=jnp.float32)
        total += main[:all_rows] + main[all_rows:] + cross
    return [total[b * rows : (b + 1) * rows] for b in range(len(blocks))]


def slots_kernel(blocks_count, parts_count, places, *refs):
    blocks, refs = refs[:blocks_count], refs[blocks_count:]
    high, low, *refs = refs
    parts, outs = refs[:parts_count], refs[parts_count:]
    rows, columns = blocks[0].shape[0], high.shape[1]
    totals = products(blocks, high, low)
    start = pl.multiple_of(places[0], columns)
    ahead = lax.broadcasted_iota(jnp.int32, (rows, columns), 1)
    ahead -= lax.broadcasted_iota(jnp.int32, (rows, columns), 0)
    for b, block in enumerate(blocks):
        current = block[:, pl.ds(start, columns)]
        mask = ahead == places[1 + b]
        inverse = step_size / jnp.where(mask, current, 1.0)
        totals[b] += jnp.where(mask, inverse, 0.0)
    if len(outs) == blocks_count:
        for out, value in zip(outs, totals):
            out[...] = value
        return
    per_out = outs[0].shape[0] // rows
    for o, out in enumerate(outs):
        for b in range(per_out):
            found = jnp.zeros((rows, columns), jnp.float32)
            for position, value in enumerate([part[...] for part in parts] + totals):
                mine = places[1 + blocks_count + position] == o * per_out + b
                found = found + jnp.where(mine, value, 0.0)
            out[b * rows : (b + 1) * rows] = found


def last_kernel(first_k, masks, block, high, low, *refs):
    shares, outs = refs[: len(refs) // 2], refs[len(refs) // 2 :]
    rows = block.shape[0]
    (total,) = products([block], high, low, first_k)
    for o, out in enumerate(outs):
        for b in range(out.shape[0] // rows):
            span = slice(b * rows, (b + 1) * rows)
            out[span] = shares[o][span] + jnp.where(masks[o, span] != 0, total, 0.0)


def final_kernel(diagonal, *refs):
    *terms, out = refs
    moved = sum_of([term[...] for term in terms])
    limit = step_size * penalty
    shrunk = jnp.maximum(moved - limit, 0.0) + jnp.minimum(moved + limit, 0.0)
    out[...] = jnp.where(diagonal[...] != 0, moved, shrunk)


def call(kernel, count, shape, scalars, arrays, limit):
    return pl.pallas_call(
        kernel,
        out_shape=[jax.ShapeDtypeStruct(shape, jnp.float32)] * count,
        in_specs=[pl.BlockSpec(memory_space=pltpu.SMEM)] * len(scalars)
        + [pl.BlockSpec(memory_space=pltpu.VMEM)] * len(arrays),
        out_specs=[pl.BlockSpec(memory_space=pltpu.VMEM)] * count,
        compiler_params=pltpu.CompilerParams(vmem_limit_bytes=limit * 1024 * 1024),
        cost_estimate=pl.CostEstimate(
            flops=0, bytes_accessed=count * shape[0] * shape[1] * 4, transcendentals=0
        ),
    )(*scalars, *arrays)


def sum_of(terms):
    total = terms[0]
    for term in terms[1:]:
        total = total + term
    return total


def per_device(omega_rows, covariance_columns, tile_offsets):
    team_count = lax.axis_size("team")
    rep_count = lax.axis_size("rep")
    team_index = lax.axis_index("team")
    rep_index = lax.axis_index("rep")
    block_rows, part_width = omega_rows.shape
    tile_width = covariance_columns.shape[1]
    all_rows = block_rows * team_count
    rows_share = all_rows // rep_count
    offset = tile_offsets[0]
    assert all_rows <= part_width and part_width % tile_width == 0
    assert rows_share % block_rows == 0 and rep_count & (rep_count - 1) == 0 and rep_count > 1

    k_ids = rep_index * part_width + jnp.arange(part_width, dtype=jnp.int32)
    c_ids = offset + jnp.arange(tile_width, dtype=jnp.int32)
    chosen = (k_ids[:, None] == c_ids[None, :]).astype(jnp.float32)
    weights = halves(chosen - step_size * covariance_columns)

    cut = part_width // 4 * 3
    assert all_rows <= cut and cut % tile_width == 0

    share_blocks = rows_share // block_rows

    def products_of(blocks, sources, spots=(), parts=()):
        start = jnp.clip(offset, 0, cut - tile_width)
        shifts = [
            jnp.where(rep_index == 0, source * block_rows - offset, 1 << 20) for source in sources
        ]
        places = jnp.stack([start, *shifts, *spots]).astype(jnp.int32)
        count, rows = (rep_count, rows_share) if spots else (len(blocks), block_rows)
        kernel = functools.partial(slots_kernel, len(blocks), len(parts))
        arrays = [*blocks, *weights, *parts]
        return call(kernel, count, (rows, tile_width), [places], arrays, 4 + len(parts) // 4)

    ring = list(range(0, team_count, 2)) + list(range(1, team_count, 2))[::-1]
    onward = [(ring[k], ring[(k + 1) % team_count]) for k in range(team_count)]
    backward = [(to, source) for source, to in onward]
    rank = team_index // 2
    place = jnp.where(team_index % 2 == 0, rank, team_count - 1 - rank)

    def device_at(spot):
        spot = spot % team_count
        up = 2 * spot
        return jnp.where(up < team_count, up, 2 * team_count - 1 - up)

    first = lax.ppermute(omega_rows, "team", onward)
    own = omega_rows
    first, *weights = lax.optimization_barrier((first, *weights))
    last_step = team_count // 2
    gathered = []
    held = first
    for step in range(2, last_step):
        held = lax.ppermute(held, "team", onward)
        gathered.append((held, step))
    last_held = held
    held = own
    for step in range(1, team_count - last_step):
        held = lax.ppermute(held, "team", backward)
        gathered.append((held, -step))

    last_left = lax.ppermute(last_held[:, :cut], "team", onward)
    last_right = lax.ppermute(last_held[:, cut:], "team", onward)
    sources = [team_index, device_at(place - 1)]
    parts = products_of([own, first], sources)
    for block, step in gathered:
        sources.append(device_at(place - step))
        parts += products_of([block], sources[-1:])
    sources.append(device_at(place - last_step))

    spots = [
        ((source // share_blocks) ^ rep_index) * share_blocks + source % share_blocks
        for source in sources
    ]
    row_spots = jnp.arange(rep_count * rows_share, dtype=jnp.int32) // block_rows
    masks = jnp.broadcast_to(
        (row_spots == spots[-1]).astype(jnp.int32).reshape(rep_count, rows_share, 1),
        (rep_count, rows_share, tile_width),
    )
    global_rows = rep_index * rows_share + jnp.arange(rows_share, dtype=jnp.int32)
    diagonal = (global_rows[:, None] == c_ids[None, :]).astype(jnp.int32)
    last_left, masks, diagonal = lax.optimization_barrier((last_left, masks, diagonal))
    shares = products_of([last_left], sources[-1:], spots, parts)
    kernel = functools.partial(last_kernel, cut)
    arrays = [masks, last_right, *weights, *shares]
    shares = call(kernel, rep_count, (rows_share, tile_width), [], arrays, 4 + rep_count)
    terms = [shares[0]]
    flips = list(range(rep_count - 1, 0, -1))
    for flip in [flips[0], *flips[:0:-1]]:
        pairs = [(d, d ^ flip) for d in range(rep_count)]
        terms.append(lax.ppermute(shares[flip], "rep", pairs))
    arrays = [diagonal, *terms]
    return call(final_kernel, 1, (rows_share, tile_width), [], arrays, 2 + rep_count)[0]


def solution(mesh):
    in_specs = (P(("groups", "team"), "rep"), P("rep", ("groups", "team")), P(("groups", "team")))
    out_specs = P("rep", ("groups", "team"))
    return jax.shard_map(
        per_device, mesh=mesh, in_specs=in_specs, out_specs=out_specs, check_vma=False
    )
```
